512 devices in a mesh: seq: 128 (over y, z, core), ch: 4 (over x).
Axes of the slice: x: 4, y: 4, z: 16, core: 2. Of those that a mesh axis runs over, the one named last changes fastest.
Arguments:
- signal: bfloat16 [16384, 4096], P('seq', 'ch'), may hold values from -6 to 6
- upstream: bfloat16 [16384, 4096], P('seq', 'ch'), may hold values from -6 to 6
- long_filter: bfloat16 [16384, 4096], P('seq', 'ch'), may hold values from -1 to 1
- short_filter: bfloat16 [128, 256], P(None, 'ch'), may hold values from -0.5 to 0.5
- skip_gain: float32 [4096], P('ch'), may hold values from 0.5 to 1.5
Outputs:
- grad_signal: bfloat16 [16384, 4096], P('seq', 'ch')
- grad_long: bfloat16 [16384, 4096], P('seq', 'ch')
- grad_short: float32 [128, 256], P(None, 'ch')
The draws below stay inside these ranges and needn't reach their ends.
All inputs are finite; a program needn't handle non-finite values.
Results may differ from the reference program's by a relative error of at most 0.012.
Values may be sent and summed in bfloat16 or wider, within the bound.
No kernel may reach another device: no remote copies, remote signals or barrier semaphores. Data moves between devices by JAX's collectives and lax.ppermute only.
A program may use at most 64 MiB of HBM per device.

```python
import math
import jax
import jax.numpy as jnp
from jax import lax

C = 4096
GROUP = 16
TAPS = 128
TOKENS = 16384
GROUPS = 256


def draw_long_filter(key, part):
    rate_key, noise_key = jax.random.split(key)
    lag_index = jnp.arange(TOKENS, dtype=jnp.float32)[:, None]
    slowest = 0.5 / TOKENS
    fastest = 1.0 / 40.0
    decay_rates = jnp.exp(jax.random.uniform(rate_key, (1, C), jnp.float32, math.log(slowest), math.log(fastest)))
    envelope = jnp.sqrt(2.0 * decay_rates) * jnp.exp(-decay_rates * lag_index)
    noise_part = jax.random.truncated_normal(noise_key, -4.0, 4.0, (TOKENS, C), jnp.float32)
    return (noise_part * envelope).astype(jnp.bfloat16)


def level_of(stream_key, dims, cuts, low, largest):
    def one(dim, blocks):
        heights = jax.random.uniform(jax.random.fold_in(jax.random.fold_in(stream_key, 6), dim), (blocks,), jnp.float32, low / len(cuts), largest / len(cuts))
        return jnp.repeat(jnp.exp(heights), dims[dim] // blocks).reshape((-1,) + (1,) * (len(dims) - dim - 1))

    loudness = one(*cuts[0])
    for cut in cuts[1:]:
        loudness = loudness * one(*cut)
    return loudness


def centred(stream_key, extent, deviation, most, cuts=(), kind=jnp.bfloat16):
    factor_of = level_of(stream_key, extent, cuts, -0.22, 0.18) if cuts else 1.0
    entries = jax.random.normal(stream_key, extent, jnp.float32) * deviation * factor_of
    return jnp.minimum(jnp.maximum(entries, -most), most).astype(kind)


def setup_inputs(seed: int = 0) -> dict:
    splits = jax.random.split(jax.random.key(seed), 6)
    signal = centred(splits[0], (TOKENS, C), 1.0, 6.0, ((0, 128), (1, 4)))
    upstream = centred(splits[1], (TOKENS, C), 1.0, 6.0, ((0, 128), (1, 4)))
    long_filter = draw_long_filter(jax.random.fold_in(splits[5], 71), 0)
    short_filter = centred(splits[3], (TAPS, GROUPS), TAPS ** -0.5, 0.5, ((1, 4),))
    skip_gain = jnp.clip(0.5 + 1.0 * jax.random.uniform(splits[4], (C,), jnp.float32) ** level_of(splits[4], (C,), ((0, 4),), -0.2, 0.2), 0.5, 1.5)
    return dict(signal=signal, upstream=upstream, long_filter=long_filter, short_filter=short_filter, skip_gain=skip_gain)


def tap_sum(values, taps_wide, ahead):
    padding = jnp.zeros((TAPS - 1, C), jnp.float32)
    if ahead:
        padded = jnp.concatenate([values, padding], axis=0)
    else:
        padded = jnp.concatenate([padding, values], axis=0)

    def accumulate(tap_index, total):
        if ahead:
            offset = tap_index
        else:
            offset = TAPS - 1 - tap_index
        piece = lax.dynamic_slice_in_dim(padded, offset, TOKENS, 0)
        return total + taps_wide[tap_index] * piece
    return lax.fori_loop(0, TAPS, accumulate, jnp.zeros((TOKENS, C), jnp.float32))

def correlate(arguments):
    cotangent, kernel, mixed_block = arguments
    length = 2 * TOKENS
    spectrum = jnp.fft.rfft(cotangent, n=length, axis=0)
    along_filter = jnp.fft.irfft(spectrum * jnp.conj(jnp.fft.rfft(kernel, n=length, axis=0)), n=length, axis=0)[:TOKENS]
    along_mixed = jnp.fft.irfft(spectrum * jnp.conj(jnp.fft.rfft(mixed_block, n=length, axis=0)), n=length, axis=0)[:TOKENS]
    return (along_filter.astype(jnp.float32), along_mixed.astype(jnp.float32))

def by_blocks(array, block_width):
    return array.reshape(TOKENS, C // block_width, block_width).transpose(1, 0, 2)

def reference(signal, upstream, long_filter, short_filter, skip_gain):
    signal_wide = signal.astype(jnp.float32)
    upstream_wide = upstream.astype(jnp.float32)
    taps_wide = jnp.repeat(short_filter.astype(jnp.float32), GROUP, axis=1)
    mixed = tap_sum(signal_wide, taps_wide, False).astype(jnp.bfloat16)
    block_width = min(C, 256)
    along_filter, along_mixed = lax.map(correlate, (by_blocks(upstream_wide, block_width), by_blocks(long_filter.astype(jnp.float32), block_width), by_blocks(mixed.astype(jnp.float32), block_width)))
    along_filter = along_filter.transpose(1, 0, 2).reshape(TOKENS, C)
    along_mixed = along_mixed.transpose(1, 0, 2).reshape(TOKENS, C)
    grad_mixed = (skip_gain[None, :] * upstream_wide + along_filter).astype(jnp.bfloat16)
    raw_long = along_mixed.astype(jnp.bfloat16)
    grad_wide = grad_mixed.astype(jnp.float32)
    grad_signal = tap_sum(grad_wide, taps_wide, True).astype(jnp.bfloat16)
    padded_signal = jnp.concatenate([jnp.zeros((TAPS - 1, C), jnp.float32), signal_wide], axis=0)

    def tap_grad(tap_index):
        start = (TAPS - 1 - tap_index).astype(jnp.int32)
        shifted = lax.dynamic_slice_in_dim(padded_signal, start, TOKENS, 0)
        per_channel = lax.optimization_barrier(jnp.sum(grad_wide * shifted, axis=0))
        return per_channel.reshape(GROUPS, GROUP).sum(axis=1)
    grad_short = lax.map(tap_grad, jnp.arange(TAPS, dtype=jnp.int32)) / jnp.sqrt(jnp.float32(GROUP * TOKENS))
    raw_wide = raw_long.astype(jnp.float32)
    long_rms = jnp.sqrt(jnp.sum(raw_wide * raw_wide) / (TOKENS * C))
    grad_long = (raw_wide / jnp.maximum(1.0, long_rms)).astype(jnp.bfloat16)
    return (grad_signal, grad_long, grad_short)
```

```python
import math

import jax
import jax.numpy as jnp
import numpy as np
from jax import lax
from jax.experimental import pallas as pl
from jax.experimental.pallas import tpu as pltpu
from jax.sharding import PartitionSpec as P

GROUP = 16
F32 = jnp.float32
BF16 = jnp.bfloat16


def split_table(table):
    high = table.astype(BF16)
    low = (table - high.astype(np.float64)).astype(BF16)
    return high, low


def dft_tables(blocks, width):
    total = 2 * blocks * width
    k1 = np.arange(blocks)[:, None] + 0.5
    b = np.arange(blocks)[None, :]
    p = np.arange(width)[None, :]
    angle = 2.0 * np.pi * k1 * b / (2 * blocks)
    enter = np.concatenate([np.cos(angle), -np.sin(angle)], axis=0)
    enter_high, enter_low = split_table(enter)
    enter_both = np.concatenate([enter_high, enter_low], axis=1)
    twist_angle = 2.0 * np.pi * k1 * p / total
    twist = np.stack([np.cos(twist_angle), -np.sin(twist_angle)]).astype(np.float32)
    inner_angle = 2.0 * np.pi * np.arange(width)[:, None] * p / width
    cosine, sine = np.cos(inner_angle), np.sin(inner_angle)
    inner = np.block([[cosine, -sine], [sine, cosine]])
    inner_back = np.block([[cosine, sine], [-sine, cosine]])
    leave = np.concatenate([np.cos(angle).T, -np.sin(angle).T], axis=1) * (2.0 / total)
    leave_both = np.concatenate(split_table(leave), axis=0)
    return enter_both, twist, np.stack(split_table(inner)), np.stack(split_table(inner_back)), leave_both


def split(value):
    high = value.astype(BF16)
    return high, (value - high.astype(F32)).astype(BF16)


def dot(left, right, dims=((1,), (0,))):
    return lax.dot_general(left, right, (dims, ((), ())), preferred_element_type=F32)


def skew(value, step):
    rows, width = value.shape
    row = lax.broadcasted_iota(jnp.int32, value.shape, 0)
    bit = 1
    while bit < rows:
        moved = pltpu.roll(value, (bit * step) % width, 1)
        value = jnp.where((row & bit) != 0, moved, value)
        bit *= 2
    return value


def spectral_kernel(
    got_ref, taps_ref, skip_ref, enter_ref, twist_ref, inner_ref, back_ref, leave_ref,
    out_ref, short_ref, square_ref, rows_ref, made_ref,
):
    blocks, lanes_in, width = got_ref.shape
    count = lanes_in // 3
    rows_ref[...] = got_ref[...].astype(F32).reshape(blocks * lanes_in, width)
    taps = taps_ref[...].astype(F32)
    nothing = jnp.zeros((1, width), F32)
    ahead = jnp.concatenate([nothing, taps], axis=1)
    mix_table = skew(jnp.broadcast_to(ahead, (2 * width, 2 * width)), 1)[:, :width].astype(BF16)
    behind = jnp.concatenate([taps, nothing], axis=1)
    unmix_table = skew(jnp.broadcast_to(behind, (width, 2 * width)), 1).astype(BF16)
    row = lax.broadcasted_iota(jnp.int32, (blocks, width), 0)
    twist_real, twist_imag = twist_ref[0], twist_ref[1]
    table = jnp.zeros((width, 2 * width), F32)
    squares = jnp.zeros((blocks, width), F32)

    for c in range(count):
        signal = rows_ref[pl.ds(c, blocks, stride=lanes_in), :]
        upstream = rows_ref[pl.ds(count + c, blocks, stride=lanes_in), :]
        kernel = rows_ref[pl.ds(2 * count + c, blocks, stride=lanes_in), :]
        before = jnp.where(row == 0, 0.0, pltpu.roll(signal, 1, 0))
        signal_pair = jnp.concatenate([before, signal], axis=1).astype(BF16)
        mixed = dot(signal_pair, mix_table).astype(BF16)
        highs, lows = [], []
        for data in (upstream.astype(BF16), kernel.astype(BF16), mixed):
            grid = dot(enter_ref[...], jnp.concatenate([data, data], axis=0))
            real, imag = grid[:blocks], grid[blocks:]
            turned = jnp.concatenate(
                [real * twist_real - imag * twist_imag, real * twist_imag + imag * twist_real], axis=1
            )
            high, low = split(turned)
            highs.append(high)
            lows.append(low)
        wide = dot(jnp.concatenate(highs + lows, axis=0), inner_ref[0])
        rest = dot(jnp.concatenate(highs, axis=0), inner_ref[1])
        spectra = []
        for i in range(3):
            here = slice(i * blocks, (i + 1) * blocks)
            there = slice((i + 3) * blocks, (i + 4) * blocks)
            total = wide[here] + (wide[there] + rest[here])
            spectra.append((total[:, :width], total[:, width:]))
        up_real, up_imag = spectra[0]
        highs, lows = [], []
        for real, imag in spectra[1:]:
            product = jnp.concatenate([up_real * real + up_imag * imag, up_imag * real - up_real * imag], axis=1)
            high, low = split(product)
            highs.append(high)
            lows.append(low)
        wide = dot(jnp.concatenate(highs + lows, axis=0), back_ref[0])
        rest = dot(jnp.concatenate(highs, axis=0), back_ref[1])
        reals, imags = [], []
        for i in range(2):
            here = slice(i * blocks, (i + 1) * blocks)
            there = slice((i + 2) * blocks, (i + 3) * blocks)
            total = wide[here] + (wide[there] + rest[here])
            real, imag = total[:, :width], total[:, width:]
            reals.append(real * twist_real + imag * twist_imag)
            imags.append(imag * twist_real - real * twist_imag)
        high, low = split(
            jnp.concatenate([jnp.concatenate(reals, axis=1), jnp.concatenate(imags, axis=1)], axis=0)
        )
        wide = dot(leave_ref[...], high)
        result = wide[:blocks] + (wide[blocks:] + dot(leave_ref[:blocks], low))
        raw = result[:, width:].astype(BF16).astype(F32)
        made_ref[pl.ds(c, blocks, stride=2 * count), :] = raw
        squares = squares + raw * raw
        grad = (skip_ref[0, c] * upstream + result[:, :width]).astype(BF16)
        grad_wide = grad.astype(F32)
        after = jnp.where(row == blocks - 1, 0.0, pltpu.roll(grad_wide, blocks - 1, 0))
        grad_pair = jnp.concatenate([grad, after.astype(BF16)], axis=1)
        made_ref[pl.ds(count + c, blocks, stride=2 * count), :] = dot(grad_pair, unmix_table, ((1,), (1,)))
        table = table + dot(grad, signal_pair, ((0,), (0,)))

    out_ref[...] = made_ref[...].reshape(out_ref.shape).astype(BF16)
    lined = skew(pltpu.roll(table, 2 * width - 1, 1), -1)[:, :width]
    short_ref[...] = jnp.broadcast_to(jnp.sum(lined, axis=0, keepdims=True), short_ref.shape)
    square_ref[...] = jnp.broadcast_to(jnp.sum(squares, axis=(0, 1), keepdims=True), square_ref.shape)


def spectral(got, taps, skip):
    blocks, lanes_in, width = got.shape
    count = lanes_in // 3
    vmem = pl.BlockSpec(memory_space=pltpu.VMEM)
    tables = dft_tables(blocks, width)
    return pl.pallas_call(
        spectral_kernel,
        out_shape=(
            jax.ShapeDtypeStruct((blocks, 2 * count, width), BF16),
            jax.ShapeDtypeStruct((8, width), F32),
            jax.ShapeDtypeStruct((8, width), F32),
        ),
        in_specs=[vmem, vmem, pl.BlockSpec(memory_space=pltpu.SMEM)] + [vmem] * 5,
        out_specs=(vmem, vmem, vmem),
        scratch_shapes=[
            pltpu.VMEM((blocks * lanes_in, width), F32),
            pltpu.VMEM((blocks * 2 * count, width), F32),
        ],
        compiler_params=pltpu.CompilerParams(vmem_limit_bytes=40 * 2**20),
        cost_estimate=pl.CostEstimate(flops=6 * 10**9, bytes_accessed=4 * 10**6, transcendentals=0),
    )(got, taps, skip, *[jnp.asarray(t) for t in tables])


def pieces(value):
    first = value.astype(BF16)
    rest = value - first.astype(F32)
    second = rest.astype(BF16)
    third = (rest - second.astype(F32)).astype(BF16)
    return first, second, third


def on_device(signal, upstream, long_filter, short_filter, skip_gain):
    rows, channels = signal.shape
    parts = lax.axis_size("seq")
    here = lax.axis_index("seq")
    slabs = lax.axis_size("ch")
    count = channels // parts
    tap_count, groups = short_filter.shape

    def by_owner(array):
        return array.T.reshape(parts, count, rows)

    sent = jnp.concatenate([by_owner(signal), by_owner(upstream), by_owner(long_filter)], axis=1)
    got = lax.all_to_all(sent, "seq", 0, 0, tiled=True)
    group = here * count // GROUP
    taps = lax.dynamic_slice_in_dim(short_filter.T, group, 1, 0)
    skip = lax.dynamic_slice_in_dim(skip_gain, here * count, count)[None, :]
    made, short_part, square_part = spectral(got, taps, skip)

    first, second, third = pieces(square_part[0])
    lane = lax.broadcasted_iota(jnp.int32, (rows,), 0)
    stat = jnp.where(lane == 0, first, jnp.where(lane == 1, second, third))
    short_first, short_second, _ = pieces(short_part[0])
    extra = jnp.stack([short_first, short_second, stat, stat]).reshape(1, 2, 2, rows)
    back = jnp.concatenate(
        [made.reshape(parts, count, 2, rows), jnp.broadcast_to(extra, (parts, 2, 2, rows))], axis=1
    )
    back = lax.all_to_all(back, "seq", 0, 0, tiled=True)
    stats = back[:, count + 1, 0, :3].astype(F32)
    square_total = jnp.broadcast_to(jnp.sum(stats), (8, 128))
    others = [
        lax.ppermute(square_total, "ch", [(i, (i + step) % slabs) for i in range(slabs)])
        for step in range(1, slabs)
    ]
    raw = back[:, : count // 2].reshape(channels, rows)
    grad_signal = back[:, count // 2 : count].reshape(channels, rows).T
    short = back[:, count, 0].astype(F32) + back[:, count, 1].astype(F32)
    short = jnp.sum(short.reshape(groups, parts // groups, tap_count), axis=1)
    grad_short = jnp.flip(short, axis=1).T / jnp.sqrt(jnp.float32(GROUP * rows * parts))
    for other in others:
        square_total = square_total + other
    long_rms = jnp.sqrt(square_total[0, 0] / (rows * parts * channels * slabs))
    grad_long = (raw.astype(F32) / jnp.maximum(1.0, long_rms)).astype(BF16).T
    return (grad_signal, grad_long, grad_short)


def solution(mesh):
    placed = (P("seq", "ch"), P("seq", "ch"), P("seq", "ch"), P(None, "ch"), P("ch"))
    return jax.shard_map(
        on_device,
        mesh=mesh,
        in_specs=placed,
        out_specs=(P("seq", "ch"), P("seq", "ch"), P(None, "ch")),
        check_vma=False,
    )
```

```python
import math

import jax
import jax.numpy as jnp
import numpy as np
from jax import lax
from jax.experimental import pallas as pl
from jax.experimental.pallas import tpu as pltpu
from jax.sharding import PartitionSpec as P

GROUP = 16
F32 = jnp.float32
BF16 = jnp.bfloat16


def split_table(table):
    high = table.astype(BF16)
    low = (table - high.astype(np.float64)).astype(BF16)
    return high, low


def dft_tables(blocks, width):
    total = 2 * blocks * width
    k1 = np.arange(blocks)[:, None] + 0.5
    b = np.arange(blocks)[None, :]
    p = np.arange(width)[None, :]
    angle = 2.0 * np.pi * k1 * b / (2 * blocks)
    enter = np.concatenate([np.cos(angle), -np.sin(angle)], axis=0)
    enter_high, enter_low = split_table(enter)
    enter_both = np.concatenate([enter_high, enter_low], axis=1)
    twist_angle = 2.0 * np.pi * k1 * p / total
    twist = np.stack([np.cos(twist_angle), -np.sin(twist_angle)]).astype(np.float32)
    inner_angle = 2.0 * np.pi * np.arange(width)[:, None] * p / width
    cosine, sine = np.cos(inner_angle), np.sin(inner_angle)
    inner = np.block([[cosine, -sine], [sine, cosine]])
    inner_back = np.block([[cosine, sine], [-sine, cosine]])
    leave = np.concatenate([np.cos(angle).T, -np.sin(angle).T], axis=1) * (2.0 / total)
    leave_both = np.concatenate(split_table(leave), axis=0)
    return enter_both, twist, np.stack(split_table(inner)), np.stack(split_table(inner_back)), leave_both


def split(value):
    high = value.astype(BF16)
    return high, (value - high.astype(F32)).astype(BF16)


def dot(left, right, dims=((1,), (0,))):
    return lax.dot_general(left, right, (dims, ((), ())), preferred_element_type=F32)


def skew(value, step):
    rows, width = value.shape
    row = lax.broadcasted_iota(jnp.int32, value.shape, 0)
    bit = 1
    while bit < rows:
        moved = pltpu.roll(value, (bit * step) % width, 1)
        value = jnp.where((row & bit) != 0, moved, value)
        bit *= 2
    return value


def spectral_kernel(
    got_ref, taps_ref, skip_ref, enter_ref, twist_ref, inner_ref, back_ref, leave_ref,
    out_ref, rows_ref, made_ref,
):
    blocks, lanes_in, width = got_ref.shape
    count = lanes_in // 3
    lanes_out = 2 * count + 2
    rows_ref[...] = got_ref[...].astype(F32).reshape(blocks * lanes_in, width)
    taps = taps_ref[...].astype(F32)
    nothing = jnp.zeros((1, width), F32)
    ahead = jnp.concatenate([nothing, taps], axis=1)
    mix_table = skew(jnp.broadcast_to(ahead, (2 * width, 2 * width)), 1)[:, :width].astype(BF16)
    behind = jnp.concatenate([taps, nothing], axis=1)
    unmix_table = skew(jnp.broadcast_to(behind, (width, 2 * width)), 1).astype(BF16)
    row = lax.broadcasted_iota(jnp.int32, (blocks, width), 0)
    twist_real, twist_imag = twist_ref[0], twist_ref[1]
    table = jnp.zeros((width, 2 * width), F32)
    squares = jnp.zeros((blocks, width), F32)

    for c in range(count):
        signal = rows_ref[pl.ds(c, blocks, stride=lanes_in), :]
        upstream = rows_ref[pl.ds(count + c, blocks, stride=lanes_in), :]
        kernel = rows_ref[pl.ds(2 * count + c, blocks, stride=lanes_in), :]
        before = jnp.where(row == 0, 0.0, pltpu.roll(signal, 1, 0))
        signal_pair = jnp.concatenate([before, signal], axis=1).astype(BF16)
        mixed = dot(signal_pair, mix_table).astype(BF16)
        highs, lows = [], []
        for data in (upstream.astype(BF16), kernel.astype(BF16), mixed):
            grid = dot(enter_ref[...], jnp.concatenate([data, data], axis=0))
            real, imag = grid[:blocks], grid[blocks:]
            turned = jnp.concatenate(
                [real * twist_real - imag * twist_imag, real * twist_imag + imag * twist_real], axis=1
            )
            high, low = split(turned)
            highs.append(high)
            lows.append(low)
        wide = dot(jnp.concatenate(highs + lows, axis=0), inner_ref[0])
        rest = dot(jnp.concatenate(highs, axis=0), inner_ref[1])
        spectra = []
        for i in range(3):
            here = slice(i * blocks, (i + 1) * blocks)
            there = slice((i + 3) * blocks, (i + 4) * blocks)
            total = wide[here] + (wide[there] + rest[here])
            spectra.append((total[:, :width], total[:, width:]))
        up_real, up_imag = spectra[0]
        highs, lows = [], []
        for real, imag in spectra[1:]:
            product = jnp.concatenate([up_real * real + up_imag * imag, up_imag * real - up_real * imag], axis=1)
            high, low = split(product)
            highs.append(high)
            lows.append(low)
        wide = dot(jnp.concatenate(highs + lows, axis=0), back_ref[0])
        rest = dot(jnp.concatenate(highs, axis=0), back_ref[1])
        reals, imags = [], []
        for i in range(2):
            here = slice(i * blocks, (i + 1) * blocks)
            there = slice((i + 2) * blocks, (i + 3) * blocks)
            total = wide[here] + (wide[there] + rest[here])
            real, imag = total[:, :width], total[:, width:]
            reals.append(real * twist_real + imag * twist_imag)
            imags.append(imag * twist_real - real * twist_imag)
        high, low = split(
            jnp.concatenate([jnp.concatenate(reals, axis=1), jnp.concatenate(imags, axis=1)], axis=0)
        )
        wide = dot(leave_ref[...], high)
        result = wide[:blocks] + (wide[blocks:] + dot(leave_ref[:blocks], low))
        raw = result[:, width:].astype(BF16).astype(F32)
        made_ref[pl.ds(c, blocks, stride=lanes_out), :] = raw
        squares = squares + raw * raw
        grad = (skip_ref[0, c] * upstream + result[:, :width]).astype(BF16)
        grad_wide = grad.astype(F32)
        after = jnp.where(row == blocks - 1, 0.0, pltpu.roll(grad_wide, blocks - 1, 0))
        grad_pair = jnp.concatenate([grad, after.astype(BF16)], axis=1)
        made_ref[pl.ds(count + c, blocks, stride=lanes_out), :] = dot(grad_pair, unmix_table, ((1,), (1,)))
        table = table + dot(grad, signal_pair, ((0,), (0,)))

    turned = table.T
    source = lax.broadcasted_iota(jnp.int32, turned.shape, 0)
    place = lax.broadcasted_iota(jnp.int32, turned.shape, 1)
    inside = jnp.logical_and(place < source, source <= place + width)
    lined = skew(jnp.where(inside, turned, 0.0), -1)
    short = jnp.sum(lined, axis=0, keepdims=True)
    short_high = short.astype(BF16).astype(F32)
    square = jnp.broadcast_to(jnp.sum(squares, axis=(0, 1), keepdims=True), (1, width))
    square_high = square.astype(BF16).astype(F32)
    lane = lax.broadcasted_iota(jnp.int32, (1, width), 1)
    second = jnp.where(lane == 0, square_high, jnp.where(lane == 1, square - square_high, short - short_high))
    made_ref[pl.ds(2 * count, blocks, stride=lanes_out), :] = jnp.broadcast_to(short_high, (blocks, width))
    made_ref[pl.ds(2 * count + 1, blocks, stride=lanes_out), :] = jnp.broadcast_to(second, (blocks, width))
    out_ref[...] = made_ref[...].reshape(out_ref.shape).astype(BF16)


def spectral(got, taps, skip):
    blocks, lanes_in, width = got.shape
    count = lanes_in // 3
    vmem = pl.BlockSpec(memory_space=pltpu.VMEM)
    tables = dft_tables(blocks, width)
    return pl.pallas_call(
        spectral_kernel,
        out_shape=jax.ShapeDtypeStruct((blocks, count + 1, 2, width), BF16),
        in_specs=[vmem, vmem, pl.BlockSpec(memory_space=pltpu.SMEM)] + [vmem] * 5,
        out_specs=vmem,
        scratch_shapes=[
            pltpu.VMEM((blocks * lanes_in, width), F32),
            pltpu.VMEM((blocks * (2 * count + 2), width), F32),
        ],
        compiler_params=pltpu.CompilerParams(vmem_limit_bytes=40 * 2**20),
        cost_estimate=pl.CostEstimate(flops=6 * 10**9, bytes_accessed=4 * 10**6, transcendentals=0),
    )(got, taps, skip, *[jnp.asarray(t) for t in tables])


def pack_kernel(first_ref, second_ref, third_ref, out_ref, held_ref, sems):
    owners, lanes_out, rows = out_ref.shape
    count = lanes_out // 3
    copies = [
        pltpu.make_async_copy(ref, held_ref.at[i], sems.at[i])
        for i, ref in enumerate((first_ref, second_ref, third_ref))
    ]
    for copy in copies:
        copy.start()
    for i, copy in enumerate(copies):
        copy.wait()
        out_ref[:, i * count : (i + 1) * count, :] = held_ref[i].T.reshape(owners, count, rows)


def pack(first, second, third, owners):
    rows, channels = first.shape
    hbm = pl.BlockSpec(memory_space=pl.ANY)
    return pl.pallas_call(
        pack_kernel,
        out_shape=jax.ShapeDtypeStruct((owners, 3 * channels // owners, rows), BF16),
        in_specs=[hbm] * 3,
        out_specs=pl.BlockSpec(memory_space=pltpu.VMEM),
        scratch_shapes=[pltpu.VMEM((3, rows, channels), BF16), pltpu.SemaphoreType.DMA((3,))],
        compiler_params=pltpu.CompilerParams(vmem_limit_bytes=60 * 2**20),
        cost_estimate=pl.CostEstimate(flops=10**6, bytes_accessed=6 * rows * channels * 2, transcendentals=0),
    )(first, second, third)


def square_kernel(back_ref, out_ref):
    last = back_ref.shape[1] - 1
    extra = back_ref[:, last].astype(F32)[:, 1]
    lane = lax.broadcasted_iota(jnp.int32, extra.shape, 1)
    total = jnp.sum(jnp.where(lane < 2, extra, 0.0), axis=(0, 1), keepdims=True)
    out_ref[...] = jnp.broadcast_to(total[None], out_ref.shape)


def square_sum(back, slabs):
    vmem = pl.BlockSpec(memory_space=pltpu.VMEM)
    return pl.pallas_call(
        square_kernel,
        out_shape=jax.ShapeDtypeStruct((slabs, 8, 128), F32),
        in_specs=[vmem],
        out_specs=vmem,
        compiler_params=pltpu.CompilerParams(vmem_limit_bytes=16 * 2**20),
    )(back)


def signal_kernel(scale, back_ref, signal_ref, short_ref):
    parts, pairs, _, rows = back_ref.shape
    half = (pairs - 1) // 2
    channels = signal_ref.shape[1]
    groups = short_ref.shape[0]
    signal_ref[...] = back_ref[:, half : 2 * half].astype(F32).reshape(channels, rows).T.astype(BF16)
    extra = back_ref[:, pairs - 1].astype(F32)
    high, low = extra[:, 0], extra[:, 1]
    lane = lax.broadcasted_iota(jnp.int32, low.shape, 1)
    short = high + jnp.where(lane < 2, 0.0, low)
    short_ref[...] = jnp.sum(short.reshape(groups, parts // groups, rows), axis=1) * scale


def signal_part(back, channels, groups, scale):
    parts, pairs, _, rows = back.shape
    vmem = pl.BlockSpec(memory_space=pltpu.VMEM)
    return pl.pallas_call(
        lambda *refs: signal_kernel(scale, *refs),
        out_shape=(
            jax.ShapeDtypeStruct((rows, channels), BF16),
            jax.ShapeDtypeStruct((groups, rows), F32),
        ),
        in_specs=[vmem],
        out_specs=(vmem, vmem),
        compiler_params=pltpu.CompilerParams(vmem_limit_bytes=16 * 2**20),
        cost_estimate=pl.CostEstimate(flops=10**6, bytes_accessed=4 * rows * channels, transcendentals=0),
    )(back)


def filter_kernel(entries, back_ref, squares_ref, out_ref):
    half = (back_ref.shape[1] - 1) // 2
    rows, channels = out_ref.shape
    mean = jnp.sum(squares_ref[...], axis=0)[:1, :1] * (1.0 / entries)
    divisor = jnp.maximum(1.0, jnp.sqrt(mean))
    raw = back_ref[:, :half].astype(F32).reshape(channels, rows)
    out_ref[...] = (raw / divisor).T.astype(BF16)


def filter_part(back, squares, channels, entries):
    rows = back.shape[3]
    vmem = pl.BlockSpec(memory_space=pltpu.VMEM)
    return pl.pallas_call(
        lambda *refs: filter_kernel(entries, *refs),
        out_shape=jax.ShapeDtypeStruct((rows, channels), BF16),
        in_specs=[vmem, vmem],
        out_specs=vmem,
        compiler_params=pltpu.CompilerParams(vmem_limit_bytes=16 * 2**20),
    )(back, squares)


def on_device(signal, upstream, long_filter, short_filter, skip_gain):
    rows, channels = signal.shape
    parts = lax.axis_size("seq")
    here = lax.axis_index("seq")
    slabs = lax.axis_size("ch")
    count = channels // parts
    groups = short_filter.shape[1]

    got = lax.all_to_all(pack(signal, upstream, long_filter, parts), "seq", 0, 0, tiled=True)
    group = here * count // GROUP
    taps = lax.dynamic_slice_in_dim(short_filter.T, group, 1, 0)
    skip = lax.dynamic_slice_in_dim(skip_gain, here * count, count)[None, :]
    back = lax.all_to_all(spectral(got, taps, skip), "seq", 0, 0, tiled=True)
    squares = lax.all_to_all(square_sum(back, slabs), "ch", 0, 0, tiled=True)
    scale = 1.0 / math.sqrt(GROUP * rows * parts)
    grad_signal, short = signal_part(back, channels, groups, scale)
    grad_long = filter_part(back, squares, channels, float(rows * parts * channels * slabs))
    return (grad_signal, grad_long, short.T)


def solution(mesh):
    placed = (P("seq", "ch"), P("seq", "ch"), P("seq", "ch"), P(None, "ch"), P("ch"))
    return jax.shard_map(
        on_device,
        mesh=mesh,
        in_specs=placed,
        out_specs=(P("seq", "ch"), P("seq", "ch"), P(None, "ch")),
        check_vma=False,
    )
```

```python
import math

import jax
import jax.numpy as jnp
import numpy as np
from jax import lax
from jax.experimental import pallas as pl
from jax.experimental.pallas import tpu as pltpu
from jax.sharding import PartitionSpec as P

GROUP = 16
F32 = jnp.float32
BF16 = jnp.bfloat16


def split_table(table):
    high = table.astype(BF16)
    low = (table - high.astype(np.float64)).astype(BF16)
    return high, low


def dft_tables(blocks, width):
    total = 2 * blocks * width
    k1 = np.arange(blocks)[:, None] + 0.5
    b = np.arange(blocks)[None, :]
    p = np.arange(width)[None, :]
    angle = 2.0 * np.pi * k1 * b / (2 * blocks)
    enter = np.concatenate([np.cos(angle), -np.sin(angle)], axis=0)
    enter_high, enter_low = split_table(enter)
    enter_both = np.concatenate([enter_high, enter_low], axis=1)
    twist_angle = 2.0 * np.pi * k1 * p / total
    twist = np.stack([np.cos(twist_angle), -np.sin(twist_angle)]).astype(np.float32)
    inner_angle = 2.0 * np.pi * np.arange(width)[:, None] * p / width
    cosine, sine = np.cos(inner_angle), np.sin(inner_angle)
    inner = np.block([[cosine, -sine], [sine, cosine]])
    return enter_both, twist, np.stack(split_table(inner))


def split(value):
    high = value.astype(BF16)
    return high, (value - high.astype(F32)).astype(BF16)


def dot(left, right, dims=((1,), (0,))):
    return lax.dot_general(left, right, (dims, ((), ())), preferred_element_type=F32)


def skew(value, step):
    rows, width = value.shape
    row = lax.broadcasted_iota(jnp.int32, value.shape, 0)
    bit = 1
    while bit < rows:
        moved = pltpu.roll(value, (bit * step) % width, 1)
        value = jnp.where((row & bit) != 0, moved, value)
        bit *= 2
    return value


def three(highs, lows, tables, dims=((1,), (0,))):
    high = jnp.concatenate(highs, axis=0)
    low = jnp.concatenate(lows, axis=0)
    return dot(high, tables[0], dims) + (dot(low, tables[0], dims) + dot(high, tables[1], dims))


def channel_rows(ref, first, stride, blocks):
    return ref[pl.ds(first, blocks, stride=stride), :]


def enter_grid(columns, enter_ref, twist_ref):
    blocks, width = columns[0].shape
    side = jnp.concatenate(columns, axis=1)
    grid = dot(enter_ref[...], jnp.concatenate([side, side], axis=0))
    twist_real, twist_imag = twist_ref[0], twist_ref[1]
    highs, lows = [], []
    for n in range(len(columns)):
        real = grid[:blocks, n * width : (n + 1) * width]
        imag = grid[blocks:, n * width : (n + 1) * width]
        high, low = split(
            jnp.concatenate(
                [real * twist_real - imag * twist_imag, real * twist_imag + imag * twist_real], axis=1
            )
        )
        highs.append(high)
        lows.append(low)
    return highs, lows


def correlate(lefts, rights, enter_ref, twist_ref, inner_ref):
    blocks = lefts[0].shape[0]
    width = lefts[0].shape[1] // 2
    twist_real, twist_imag = twist_ref[0], twist_ref[1]
    highs, lows = [], []
    for left, right in zip(lefts, rights):
        left_real, left_imag = left[:, :width], left[:, width:]
        real, imag = right[:, :width], right[:, width:]
        high, low = split(
            jnp.concatenate(
                [left_real * real + left_imag * imag, left_imag * real - left_real * imag], axis=1
            )
        )
        highs.append(high)
        lows.append(low)
    backs = three(highs, lows, inner_ref, ((1,), (1,)))
    reals, imags = [], []
    for n in range(len(lefts)):
        real = backs[n * blocks : (n + 1) * blocks, :width]
        imag = backs[n * blocks : (n + 1) * blocks, width:]
        reals.append(real * twist_real + imag * twist_imag)
        imags.append(imag * twist_real - real * twist_imag)
    high, low = split(jnp.concatenate([jnp.concatenate(reals, axis=1), jnp.concatenate(imags, axis=1)], axis=0))
    leave = enter_ref[...].T
    wide = dot(leave, high)
    return (wide[:blocks] + (wide[blocks:] + dot(leave[:blocks], low))) * (1.0 / (blocks * width))


def filter_side_kernel(
    got_ref, taps_ref, enter_ref, twist_ref, inner_ref,
    spectrum_ref, raw_ref, square_ref, rows_ref, made_ref,
):
    blocks, lanes_in, width = got_ref.shape
    count = lanes_in // 3
    rows_ref[...] = got_ref[...].astype(F32).reshape(blocks * lanes_in, width)
    ahead = jnp.concatenate([jnp.zeros((1, width), F32), taps_ref[...].astype(F32)], axis=1)
    mix_table = skew(jnp.broadcast_to(ahead, (2 * width, 2 * width)), 1)[:, :width].astype(BF16)
    row = lax.broadcasted_iota(jnp.int32, (blocks, width), 0)
    pairs, columns = [], []
    for c in range(count):
        signal = channel_rows(rows_ref, c, lanes_in, blocks)
        before = jnp.where(row == 0, 0.0, pltpu.roll(signal, 1, 0))
        pairs.append(jnp.concatenate([before, signal], axis=1).astype(BF16))
        columns.append(channel_rows(rows_ref, count + c, lanes_in, blocks).astype(BF16))
    mixed = dot(jnp.concatenate(pairs, axis=0), mix_table).astype(BF16)
    columns += [mixed[c * blocks : (c + 1) * blocks] for c in range(count)]
    highs, lows = enter_grid(columns, enter_ref, twist_ref)
    spectra = three(highs, lows, inner_ref)
    spectrum_ref[...] = spectra[: count * blocks]
    lefts = [spectra[c * blocks : (c + 1) * blocks] for c in range(count)]
    rights = [spectra[(count + c) * blocks : (count + c + 1) * blocks] for c in range(count)]
    result = correlate(lefts, rights, enter_ref, twist_ref, inner_ref)
    squares = jnp.zeros((blocks, width), F32)
    for c in range(count):
        raw = result[:, c * width : (c + 1) * width].astype(BF16).astype(F32)
        made_ref[pl.ds(c, blocks, stride=count), :] = raw
        squares = squares + raw * raw
    raw_ref[...] = made_ref[...].reshape(raw_ref.shape).astype(BF16)
    total = jnp.sum(squares, axis=(0, 1), keepdims=True)
    square_ref[...] = jnp.broadcast_to(total[None], square_ref.shape)


def signal_side_kernel(
    got_ref, spectrum_ref, raw_ref, taps_ref, skip_ref, enter_ref, twist_ref, inner_ref,
    out_ref, short_ref, rows_ref, made_ref,
):
    blocks, pairs_out, _, width = out_ref.shape
    count = pairs_out - 1
    lanes_in = 3 * count
    rows_ref[...] = got_ref[...].astype(F32).reshape(blocks * lanes_in, width)
    behind = jnp.concatenate([taps_ref[...].astype(F32), jnp.zeros((1, width), F32)], axis=1)
    unmix_table = skew(jnp.broadcast_to(behind, (width, 2 * width)), 1).astype(BF16)
    row = lax.broadcasted_iota(jnp.int32, (blocks, width), 0)
    columns = [channel_rows(rows_ref, 2 * count + c, lanes_in, blocks).astype(BF16) for c in range(count)]
    highs, lows = enter_grid(columns, enter_ref, twist_ref)
    spectra = three(highs, lows, inner_ref)
    lefts = [spectrum_ref[c * blocks : (c + 1) * blocks, :] for c in range(count)]
    rights = [spectra[c * blocks : (c + 1) * blocks] for c in range(count)]
    result = correlate(lefts, rights, enter_ref, twist_ref, inner_ref)
    pairs, grads, signals = [], [], []
    for c in range(count):
        upstream = channel_rows(rows_ref, count + c, lanes_in, blocks)
        grad = (skip_ref[0, c] * upstream + result[:, c * width : (c + 1) * width]).astype(BF16)
        after = jnp.where(row == blocks - 1, 0.0, pltpu.roll(grad.astype(F32), blocks - 1, 0))
        pairs.append(jnp.concatenate([grad, after.astype(BF16)], axis=1))
        grads.append(grad)
        signal = channel_rows(rows_ref, c, lanes_in, blocks)
        before = jnp.where(row == 0, 0.0, pltpu.roll(signal, 1, 0))
        signals.append(jnp.concatenate([before, signal], axis=1).astype(BF16))
    made = dot(jnp.concatenate(pairs, axis=0), unmix_table, ((1,), (1,)))
    for c in range(count):
        made_ref[pl.ds(c, blocks, stride=count), :] = made[c * blocks : (c + 1) * blocks]
    half = count // 2
    out_ref[:, :half] = raw_ref[...]
    out_ref[:, half:count] = made_ref[...].reshape(blocks, half, 2, width).astype(BF16)
    out_ref[:, count:] = jnp.zeros((blocks, 1, 2, width), BF16)
    table = dot(jnp.concatenate(grads, axis=0), jnp.concatenate(signals, axis=0), ((0,), (0,)))
    turned = table.T
    source = lax.broadcasted_iota(jnp.int32, turned.shape, 0)
    place = lax.broadcasted_iota(jnp.int32, turned.shape, 1)
    inside = jnp.logical_and(place < source, source <= place + width)
    lined = skew(jnp.where(inside, turned, 0.0), -1)
    short_ref[...] = jnp.broadcast_to(jnp.sum(lined, axis=0, keepdims=True), short_ref.shape)


def filter_side(got, taps, tables, slabs):
    blocks, lanes_in, width = got.shape
    count = lanes_in // 3
    vmem = pl.BlockSpec(memory_space=pltpu.VMEM)
    return pl.pallas_call(
        filter_side_kernel,
        out_shape=(
            jax.ShapeDtypeStruct((count * blocks, 2 * width), F32),
            jax.ShapeDtypeStruct((blocks, count // 2, 2, width), BF16),
            jax.ShapeDtypeStruct((slabs, 8, width), F32),
        ),
        in_specs=[vmem] * 5,
        out_specs=(vmem,) * 3,
        scratch_shapes=[
            pltpu.VMEM((blocks * lanes_in, width), F32),
            pltpu.VMEM((blocks * count, width), F32),
        ],
        compiler_params=pltpu.CompilerParams(vmem_limit_bytes=40 * 2**20),
        cost_estimate=pl.CostEstimate(flops=3 * 10**9, bytes_accessed=6 * 10**6, transcendentals=0),
    )(got, taps, *tables)


def signal_side(got, spectrum, raw, taps, skip, tables):
    blocks, lanes_in, width = got.shape
    count = lanes_in // 3
    vmem = pl.BlockSpec(memory_space=pltpu.VMEM)
    return pl.pallas_call(
        signal_side_kernel,
        out_shape=(
            jax.ShapeDtypeStruct((blocks, count + 1, 2, width), BF16),
            jax.ShapeDtypeStruct((8, width), F32),
        ),
        in_specs=[vmem] * 4 + [pl.BlockSpec(memory_space=pltpu.SMEM)] + [vmem] * 3,
        out_specs=(vmem, vmem),
        scratch_shapes=[
            pltpu.VMEM((blocks * lanes_in, width), F32),
            pltpu.VMEM((blocks * count, width), F32),
        ],
        compiler_params=pltpu.CompilerParams(vmem_limit_bytes=40 * 2**20),
        cost_estimate=pl.CostEstimate(flops=3 * 10**9, bytes_accessed=6 * 10**6, transcendentals=0),
    )(got, spectrum, raw, taps, skip, *tables)


def stamp_kernel(message_ref, short_ref, squares_ref, out_ref, extra_ref, sem):
    del message_ref
    blocks, _, width = extra_ref.shape
    short = short_ref[:1, :]
    short_high = short.astype(BF16).astype(F32)
    square = jnp.sum(squares_ref[...], axis=0)[:1, :]
    square_high = square.astype(BF16).astype(F32)
    lane = lax.broadcasted_iota(jnp.int32, (1, width), 1)
    rest = jnp.where(lane == 0, square_high, jnp.where(lane == 1, square - square_high, short - short_high))
    both = jnp.concatenate([short_high, rest], axis=0)
    extra_ref[...] = jnp.broadcast_to(both[None], extra_ref.shape).astype(BF16)
    copy = pltpu.make_async_copy(extra_ref, out_ref.at[:, out_ref.shape[1] - 1], sem)
    copy.start()
    copy.wait()


def stamp(message, short, squares):
    blocks, _, _, width = message.shape
    vmem = pl.BlockSpec(memory_space=pltpu.VMEM)
    hbm = pl.BlockSpec(memory_space=pl.ANY)
    return pl.pallas_call(
        stamp_kernel,
        out_shape=jax.ShapeDtypeStruct(message.shape, BF16),
        in_specs=[hbm, vmem, vmem],
        out_specs=hbm,
        input_output_aliases={0: 0},
        scratch_shapes=[pltpu.VMEM((blocks, 2, width), BF16), pltpu.SemaphoreType.DMA],
        compiler_params=pltpu.CompilerParams(vmem_limit_bytes=8 * 2**20),
    )(message, short, squares)


def pack_kernel(first_ref, second_ref, third_ref, out_ref, held_ref, sems):
    owners, lanes_out, rows = out_ref.shape
    count = lanes_out // 3
    copies = [
        pltpu.make_async_copy(ref, held_ref.at[i], sems.at[i])
        for i, ref in enumerate((first_ref, second_ref, third_ref))
    ]
    for copy in copies:
        copy.start()
    for i, copy in enumerate(copies):
        copy.wait()
        out_ref[:, i * count : (i + 1) * count, :] = held_ref[i].T.reshape(owners, count, rows)


def pack(first, second, third, owners):
    rows, channels = first.shape
    hbm = pl.BlockSpec(memory_space=pl.ANY)
    return pl.pallas_call(
        pack_kernel,
        out_shape=jax.ShapeDtypeStruct((owners, 3 * channels // owners, rows), BF16),
        in_specs=[hbm] * 3,
        out_specs=pl.BlockSpec(memory_space=pltpu.VMEM),
        scratch_shapes=[pltpu.VMEM((3, rows, channels), BF16), pltpu.SemaphoreType.DMA((3,))],
        compiler_params=pltpu.CompilerParams(vmem_limit_bytes=60 * 2**20),
        cost_estimate=pl.CostEstimate(flops=10**6, bytes_accessed=6 * rows * channels * 2, transcendentals=0),
    )(first, second, third)


def finish_kernel(entries, scale, back_ref, signal_ref, filter_ref, short_ref):
    parts, pairs, _, rows = back_ref.shape
    half = (pairs - 1) // 2
    channels = signal_ref.shape[1]
    groups = short_ref.shape[0]
    extra = back_ref[:, pairs - 1].astype(F32)
    high, low = extra[:, 0], extra[:, 1]
    lane = lax.broadcasted_iota(jnp.int32, low.shape, 1)
    short = high + jnp.where(lane < 2, 0.0, low)
    short_ref[...] = jnp.sum(short.reshape(groups, parts // groups, rows), axis=1) * scale
    squares = jnp.sum(jnp.where(lane < 2, low, 0.0), axis=(0, 1), keepdims=True)
    divisor = jnp.maximum(1.0, jnp.sqrt(squares * (1.0 / entries)))
    signal_ref[...] = back_ref[:, half : 2 * half].astype(F32).reshape(channels, rows).T.astype(BF16)
    raw = back_ref[:, :half].astype(F32).reshape(channels, rows)
    filter_ref[...] = (raw / divisor).T.astype(BF16)


def finish(back, channels, groups, entries, scale):
    rows = back.shape[3]
    vmem = pl.BlockSpec(memory_space=pltpu.VMEM)
    return pl.pallas_call(
        lambda *refs: finish_kernel(entries, scale, *refs),
        out_shape=(
            jax.ShapeDtypeStruct((rows, channels), BF16),
            jax.ShapeDtypeStruct((rows, channels), BF16),
            jax.ShapeDtypeStruct((groups, rows), F32),
        ),
        in_specs=[vmem],
        out_specs=(vmem, vmem, vmem),
        compiler_params=pltpu.CompilerParams(vmem_limit_bytes=16 * 2**20),
    )(back)


def on_device(signal, upstream, long_filter, short_filter, skip_gain):
    rows, channels = signal.shape
    parts = lax.axis_size("seq")
    here = lax.axis_index("seq")
    slabs = lax.axis_size("ch")
    count = channels // parts
    groups = short_filter.shape[1]
    tables = [jnp.asarray(table) for table in dft_tables(parts, rows)]

    got = lax.all_to_all(pack(signal, upstream, long_filter, parts), "seq", 0, 0, tiled=True)
    group = here * count // GROUP
    taps = lax.dynamic_slice_in_dim(short_filter.T, group, 1, 0)
    skip = lax.dynamic_slice_in_dim(skip_gain, here * count, count)[None, :]
    spectrum, raw, squares = filter_side(got, taps, tables, slabs)
    squares = lax.all_to_all(squares, "ch", 0, 0, tiled=True)
    message, short = signal_side(got, spectrum, raw, taps, skip, tables)
    back = lax.all_to_all(stamp(message, short, squares), "seq", 0, 0, tiled=True)
    entries = float(rows * parts * channels * slabs)
    scale = 1.0 / math.sqrt(GROUP * rows * parts)
    grad_signal, grad_long, short = finish(back, channels, groups, entries, scale)
    return (grad_signal, grad_long, short.T)


def solution(mesh):
    placed = (P("seq", "ch"), P("seq", "ch"), P("seq", "ch"), P(None, "ch"), P("ch"))
    return jax.shard_map(
        on_device,
        mesh=mesh,
        in_specs=placed,
        out_specs=(P("seq", "ch"), P("seq", "ch"), P(None, "ch")),
        check_vma=False,
    )
```

```python
import math

import jax
import jax.numpy as jnp
import numpy as np
from jax import lax
from jax.experimental import pallas as pl
from jax.experimental.pallas import tpu as pltpu
from jax.sharding import PartitionSpec as P

GROUP = 16
F32 = jnp.float32
BF16 = jnp.bfloat16


def split_table(table):
    high = table.astype(BF16)
    low = (table - high.astype(np.float64)).astype(BF16)
    return high, low


def dft_tables(blocks, width):
    total = 2 * blocks * width
    k1 = np.arange(blocks)[:, None] + 0.5
    b = np.arange(blocks)[None, :]
    p = np.arange(width)[None, :]
    angle = 2.0 * np.pi * k1 * b / (2 * blocks)
    enter = np.concatenate([np.cos(angle), -np.sin(angle)], axis=0)
    enter_high, enter_low = split_table(enter)
    enter_both = np.concatenate([enter_high, enter_low], axis=1)
    twist_angle = 2.0 * np.pi * k1 * p / total
    twist = np.stack([np.cos(twist_angle), -np.sin(twist_angle)]).astype(np.float32)
    inner_angle = 2.0 * np.pi * np.arange(width)[:, None] * p / width
    cosine, sine = np.cos(inner_angle), np.sin(inner_angle)
    inner = np.block([[cosine, -sine], [sine, cosine]])
    return enter_both, twist, np.stack(split_table(inner))


def split(value):
    high = value.astype(BF16)
    return high, (value - high.astype(F32)).astype(BF16)


def dot(left, right, dims=((1,), (0,))):
    return lax.dot_general(left, right, (dims, ((), ())), preferred_element_type=F32)


def skew(value, step):
    rows, width = value.shape
    row = lax.broadcasted_iota(jnp.int32, value.shape, 0)
    bit = 1
    while bit < rows:
        moved = pltpu.roll(value, (bit * step) % width, 1)
        value = jnp.where((row & bit) != 0, moved, value)
        bit *= 2
    return value


def group_taps(taps_ref, count):
    group = lax.axis_index("seq") * count // GROUP
    row = lax.broadcasted_iota(jnp.int32, taps_ref.shape, 0)
    return jnp.sum(jnp.where(row == group, taps_ref[...].astype(F32), 0.0), axis=0, keepdims=True)


def slide(line, rows):
    return pltpu.roll(jnp.broadcast_to(line, (rows, line.shape[1])), 0, 1, stride=1, stride_axis=0)


def three(highs, lows, tables, dims=((1,), (0,))):
    high = jnp.concatenate(highs, axis=0)
    low = jnp.concatenate(lows, axis=0)
    return dot(high, tables[0], dims) + (dot(low, tables[0], dims) + dot(high, tables[1], dims))


def channel_rows(ref, first, stride, blocks):
    return ref[pl.ds(first, blocks, stride=stride), :]


def enter_grid(columns, enter_ref, twist_ref):
    blocks, width = columns[0].shape
    side = jnp.concatenate(columns, axis=1)
    grid = dot(enter_ref[...], jnp.concatenate([side, side], axis=0))
    twist_real, twist_imag = twist_ref[0], twist_ref[1]
    highs, lows = [], []
    for n in range(len(columns)):
        real = grid[:blocks, n * width : (n + 1) * width]
        imag = grid[blocks:, n * width : (n + 1) * width]
        high, low = split(
            jnp.concatenate(
                [real * twist_real - imag * twist_imag, real * twist_imag + imag * twist_real], axis=1
            )
        )
        highs.append(high)
        lows.append(low)
    return highs, lows


def correlate(lefts, rights, enter_ref, twist_ref, inner_ref):
    blocks = lefts[0].shape[0]
    width = lefts[0].shape[1] // 2
    twist_real, twist_imag = twist_ref[0], twist_ref[1]
    highs, lows = [], []
    for left, right in zip(lefts, rights):
        left_real, left_imag = left[:, :width], left[:, width:]
        real, imag = right[:, :width], right[:, width:]
        high, low = split(
            jnp.concatenate(
                [left_real * real + left_imag * imag, left_imag * real - left_real * imag], axis=1
            )
        )
        highs.append(high)
        lows.append(low)
    backs = three(highs, lows, inner_ref, ((1,), (1,)))
    reals, imags = [], []
    for n in range(len(lefts)):
        real = backs[n * blocks : (n + 1) * blocks, :width]
        imag = backs[n * blocks : (n + 1) * blocks, width:]
        reals.append(real * twist_real + imag * twist_imag)
        imags.append(imag * twist_real - real * twist_imag)
    high, low = split(jnp.concatenate([jnp.concatenate(reals, axis=1), jnp.concatenate(imags, axis=1)], axis=0))
    leave = enter_ref[...].T
    wide = dot(leave, high)
    return (wide[:blocks] + (wide[blocks:] + dot(leave[:blocks], low))) * (1.0 / (blocks * width))


def filter_side_kernel(
    got_ref, taps_ref, enter_ref, twist_ref, inner_ref,
    spectrum_ref, raw_ref, square_ref, rows_ref,
):
    blocks, lanes_in, width = got_ref.shape
    count = lanes_in // 3
    lanes_here = 2 * count
    rows_ref[...] = got_ref[:, :lanes_here].astype(F32).reshape(blocks * lanes_here, width)
    ahead = jnp.concatenate([jnp.zeros((1, width), F32), group_taps(taps_ref, count)], axis=1)
    mix_table = slide(ahead, 2 * width)[:, :width].astype(BF16)
    row = lax.broadcasted_iota(jnp.int32, (blocks, width), 0)
    pairs, columns = [], []
    for c in range(count):
        signal = channel_rows(rows_ref, c, lanes_here, blocks)
        before = jnp.where(row == 0, 0.0, pltpu.roll(signal, 1, 0))
        pairs.append(jnp.concatenate([before, signal], axis=1).astype(BF16))
        columns.append(channel_rows(rows_ref, count + c, lanes_here, blocks).astype(BF16))
    mixed = dot(jnp.concatenate(pairs, axis=0), mix_table).astype(BF16)
    columns += [mixed[c * blocks : (c + 1) * blocks] for c in range(count)]
    highs, lows = enter_grid(columns, enter_ref, twist_ref)
    spectra = three(highs, lows, inner_ref)
    spectrum_ref[...] = spectra[: count * blocks]
    lefts = [spectra[c * blocks : (c + 1) * blocks] for c in range(count)]
    rights = [spectra[(count + c) * blocks : (count + c + 1) * blocks] for c in range(count)]
    result = correlate(lefts, rights, enter_ref, twist_ref, inner_ref)
    squares = jnp.zeros((blocks, width), F32)
    for c in range(count):
        raw = result[:, c * width : (c + 1) * width].astype(BF16)
        raw_ref[c] = raw
        squares = squares + raw.astype(F32) * raw.astype(F32)
    total = jnp.sum(squares, axis=(0, 1), keepdims=True)
    square_ref[...] = jnp.broadcast_to(total[None], square_ref.shape)


def signal_side_kernel(
    got_ref, spectrum_ref, raw_ref, taps_ref, skip_ref, enter_ref, twist_ref, inner_ref,
    out_ref, short_ref, rows_ref, made_ref,
):
    blocks, pairs_out, _, width = out_ref.shape
    count = pairs_out - 1
    lanes_in = 3 * count
    rows_ref[...] = got_ref[...].astype(F32).reshape(blocks * lanes_in, width)
    behind = jnp.concatenate([group_taps(taps_ref, count), jnp.zeros((1, width), F32)], axis=1)
    unmix_table = slide(behind, width).astype(BF16)
    row = lax.broadcasted_iota(jnp.int32, (blocks, width), 0)
    columns = [channel_rows(rows_ref, 2 * count + c, lanes_in, blocks).astype(BF16) for c in range(count)]
    highs, lows = enter_grid(columns, enter_ref, twist_ref)
    spectra = three(highs, lows, inner_ref)
    lefts = [spectrum_ref[c * blocks : (c + 1) * blocks, :] for c in range(count)]
    rights = [spectra[c * blocks : (c + 1) * blocks] for c in range(count)]
    result = correlate(lefts, rights, enter_ref, twist_ref, inner_ref)
    first = lax.axis_index("seq") * count
    pairs, grads, signals = [], [], []
    for c in range(count):
        upstream = channel_rows(rows_ref, count + c, lanes_in, blocks)
        grad = (skip_ref[first + c] * upstream + result[:, c * width : (c + 1) * width]).astype(BF16)
        after = jnp.where(row == blocks - 1, 0.0, pltpu.roll(grad.astype(F32), blocks - 1, 0))
        pairs.append(jnp.concatenate([grad, after.astype(BF16)], axis=1))
        grads.append(grad)
        signal = channel_rows(rows_ref, c, lanes_in, blocks)
        before = jnp.where(row == 0, 0.0, pltpu.roll(signal, 1, 0))
        signals.append(jnp.concatenate([before, signal], axis=1).astype(BF16))
    made = dot(jnp.concatenate(pairs, axis=0), unmix_table, ((1,), (1,)))
    for c in range(count):
        made_ref[pl.ds(c, blocks, stride=2 * count), :] = raw_ref[c].astype(F32)
        made_ref[pl.ds(count + c, blocks, stride=2 * count), :] = made[c * blocks : (c + 1) * blocks]
    out_ref[:, :count] = made_ref[...].reshape(blocks, count, 2, width).astype(BF16)
    out_ref[:, count:] = jnp.zeros((blocks, 1, 2, width), BF16)
    table = dot(jnp.concatenate(grads, axis=0), jnp.concatenate(signals, axis=0), ((0,), (0,)))
    turned = table.T
    source = lax.broadcasted_iota(jnp.int32, turned.shape, 0)
    place = lax.broadcasted_iota(jnp.int32, turned.shape, 1)
    inside = jnp.logical_and(place < source, source <= place + width)
    lined = skew(jnp.where(inside, turned, 0.0), -1)
    short_ref[...] = jnp.broadcast_to(jnp.sum(lined, axis=0, keepdims=True), short_ref.shape)


def filter_side(got, taps, tables, slabs):
    blocks, lanes_in, width = got.shape
    count = lanes_in // 3
    vmem = pl.BlockSpec(memory_space=pltpu.VMEM)
    return pl.pallas_call(
        filter_side_kernel,
        out_shape=(
            jax.ShapeDtypeStruct((count * blocks, 2 * width), F32),
            jax.ShapeDtypeStruct((count, blocks, width), BF16),
            jax.ShapeDtypeStruct((slabs, 8, width), F32),
        ),
        in_specs=[vmem] * 5,
        out_specs=(vmem,) * 3,
        scratch_shapes=[
            pltpu.VMEM((blocks * 2 * count, width), F32),
        ],
        compiler_params=pltpu.CompilerParams(vmem_limit_bytes=40 * 2**20),
        cost_estimate=pl.CostEstimate(flops=3 * 10**9, bytes_accessed=6 * 10**6, transcendentals=0),
    )(got, taps, *tables)


def signal_side(got, spectrum, raw, taps, skip, tables):
    blocks, lanes_in, width = got.shape
    count = lanes_in // 3
    vmem = pl.BlockSpec(memory_space=pltpu.VMEM)
    return pl.pallas_call(
        signal_side_kernel,
        out_shape=(
            jax.ShapeDtypeStruct((blocks, count + 1, 2, width), BF16),
            jax.ShapeDtypeStruct((8, width), F32),
        ),
        in_specs=[vmem] * 4 + [pl.BlockSpec(memory_space=pltpu.SMEM)] + [vmem] * 3,
        out_specs=(vmem, vmem),
        scratch_shapes=[
            pltpu.VMEM((blocks * lanes_in, width), F32),
            pltpu.VMEM((blocks * 2 * count, width), F32),
        ],
        compiler_params=pltpu.CompilerParams(vmem_limit_bytes=40 * 2**20),
        cost_estimate=pl.CostEstimate(flops=3 * 10**9, bytes_accessed=6 * 10**6, transcendentals=0),
    )(got, spectrum, raw, taps, skip, *tables)


def stamp_kernel(message_ref, short_ref, squares_ref, out_ref, extra_ref, sem):
    del message_ref
    blocks, _, width = extra_ref.shape
    short = short_ref[:1, :]
    short_high = short.astype(BF16).astype(F32)
    square = jnp.sum(squares_ref[...], axis=0)[:1, :]
    square_high = square.astype(BF16).astype(F32)
    lane = lax.broadcasted_iota(jnp.int32, (1, width), 1)
    rest = jnp.where(lane == 0, square_high, jnp.where(lane == 1, square - square_high, short - short_high))
    both = jnp.concatenate([short_high, rest], axis=0)
    extra_ref[...] = jnp.broadcast_to(both[None], extra_ref.shape).astype(BF16)
    copy = pltpu.make_async_copy(extra_ref, out_ref.at[:, out_ref.shape[1] - 1], sem)
    copy.start()
    copy.wait()


def stamp(message, short, squares):
    blocks, _, _, width = message.shape
    vmem = pl.BlockSpec(memory_space=pltpu.VMEM)
    hbm = pl.BlockSpec(memory_space=pl.ANY)
    return pl.pallas_call(
        stamp_kernel,
        out_shape=jax.ShapeDtypeStruct(message.shape, BF16),
        in_specs=[hbm, vmem, vmem],
        out_specs=hbm,
        input_output_aliases={0: 0},
        scratch_shapes=[pltpu.VMEM((blocks, 2, width), BF16), pltpu.SemaphoreType.DMA],
        compiler_params=pltpu.CompilerParams(vmem_limit_bytes=8 * 2**20),
    )(message, short, squares)


def pack_kernel(first_ref, second_ref, third_ref, out_ref, held_ref, sems):
    owners, lanes_out, rows = out_ref.shape
    count = lanes_out // 3
    copies = [
        pltpu.make_async_copy(ref, held_ref.at[i], sems.at[i])
        for i, ref in enumerate((first_ref, second_ref, third_ref))
    ]
    for copy in copies:
        copy.start()
    for i, copy in enumerate(copies):
        copy.wait()
        out_ref[:, i * count : (i + 1) * count, :] = held_ref[i].T.reshape(owners, count, rows)


def pack(first, second, third, owners):
    rows, channels = first.shape
    hbm = pl.BlockSpec(memory_space=pl.ANY)
    first, second, third = [pltpu.with_memory_space_constraint(x, pltpu.HBM) for x in (first, second, third)]
    return pl.pallas_call(
        pack_kernel,
        out_shape=jax.ShapeDtypeStruct((owners, 3 * channels // owners, rows), BF16),
        in_specs=[hbm] * 3,
        out_specs=pl.BlockSpec(memory_space=pltpu.VMEM),
        scratch_shapes=[pltpu.VMEM((3, rows, channels), BF16), pltpu.SemaphoreType.DMA((3,))],
        compiler_params=pltpu.CompilerParams(vmem_limit_bytes=16 * 2**20),
        cost_estimate=pl.CostEstimate(flops=10**6, bytes_accessed=6 * rows * channels * 2, transcendentals=0),
    )(first, second, third)


def finish_kernel(entries, scale, back_ref, signal_ref, filter_ref, short_ref):
    parts, pairs, _, rows = back_ref.shape
    half = (pairs - 1) // 2
    channels = signal_ref.shape[1]
    groups = short_ref.shape[0]
    extra = back_ref[:, pairs - 1].astype(F32)
    high, low = extra[:, 0], extra[:, 1]
    lane = lax.broadcasted_iota(jnp.int32, low.shape, 1)
    short = high + jnp.where(lane < 2, 0.0, low)
    short_ref[...] = jnp.sum(short.reshape(groups, parts // groups, rows), axis=1) * scale
    squares = jnp.sum(jnp.where(lane < 2, low, 0.0), axis=(0, 1), keepdims=True)
    divisor = jnp.maximum(1.0, jnp.sqrt(squares * (1.0 / entries)))
    signal_ref[...] = back_ref[:, half : 2 * half].astype(F32).reshape(channels, rows).T.astype(BF16)
    raw = back_ref[:, :half].astype(F32).reshape(channels, rows)
    filter_ref[...] = (raw / divisor).T.astype(BF16)


def finish(back, channels, groups, entries, scale):
    rows = back.shape[3]
    vmem = pl.BlockSpec(memory_space=pltpu.VMEM)
    return pl.pallas_call(
        lambda *refs: finish_kernel(entries, scale, *refs),
        out_shape=(
            jax.ShapeDtypeStruct((rows, channels), BF16),
            jax.ShapeDtypeStruct((rows, channels), BF16),
            jax.ShapeDtypeStruct((groups, rows), F32),
        ),
        in_specs=[vmem],
        out_specs=(vmem, vmem, vmem),
        compiler_params=pltpu.CompilerParams(vmem_limit_bytes=16 * 2**20),
    )(back)


def on_device(signal, upstream, long_filter, short_filter, skip_gain):
    rows, channels = signal.shape
    parts = lax.axis_size("seq")
    slabs = lax.axis_size("ch")
    count = channels // parts
    groups = short_filter.shape[1]
    tables = [jnp.asarray(table) for table in dft_tables(parts, rows)]

    got = lax.all_to_all(pack(signal, upstream, long_filter, parts), "seq", 0, 0, tiled=True)
    taps = short_filter.T
    spectrum, raw, squares = filter_side(got, taps, tables, slabs)
    squares = lax.all_to_all(squares, "ch", 0, 0, tiled=True)
    message, short = signal_side(got, spectrum, raw, taps, skip_gain, tables)
    back = lax.all_to_all(stamp(message, short, squares), "seq", 0, 0, tiled=True)
    entries = float(rows * parts * channels * slabs)
    scale = 1.0 / math.sqrt(GROUP * rows * parts)
    grad_signal, grad_long, short = finish(back, channels, groups, entries, scale)
    return (grad_signal, grad_long, short.T)


def solution(mesh):
    placed = (P("seq", "ch"), P("seq", "ch"), P("seq", "ch"), P(None, "ch"), P("ch"))
    return jax.shard_map(
        on_device,
        mesh=mesh,
        in_specs=placed,
        out_specs=(P("seq", "ch"), P("seq", "ch"), P(None, "ch")),
        check_vma=False,
    )
```

```python
import math

import jax
import jax.numpy as jnp
import numpy as np
from jax import lax
from jax.experimental import pallas as pl
from jax.experimental.pallas import tpu as pltpu
from jax.sharding import PartitionSpec as P

GROUP = 16
F32 = jnp.float32
BF16 = jnp.bfloat16


def split_table(table):
    high = table.astype(BF16)
    low = (table - high.astype(np.float64)).astype(BF16)
    return high, low


def dft_tables(blocks, width):
    total = 2 * blocks * width
    k1 = np.arange(blocks)[:, None] + 0.5
    b = np.arange(blocks)[None, :]
    p = np.arange(width)[None, :]
    angle = 2.0 * np.pi * k1 * b / (2 * blocks)
    enter = np.concatenate([np.cos(angle), -np.sin(angle)], axis=0)
    enter_high, enter_low = split_table(enter)
    enter_both = np.concatenate([enter_high, enter_low], axis=1)
    twist_angle = 2.0 * np.pi * k1 * p / total
    twist = np.stack([np.cos(twist_angle), -np.sin(twist_angle)]).astype(np.float32)
    inner_angle = 2.0 * np.pi * np.arange(width)[:, None] * p / width
    cosine, sine = np.cos(inner_angle), np.sin(inner_angle)
    inner = np.block([[cosine, -sine], [sine, cosine]])
    return enter_both, twist, np.stack(split_table(inner))


def split(value):
    high = value.astype(BF16)
    return high, (value - high.astype(F32)).astype(BF16)


def dot(left, right, dims=((1,), (0,))):
    return lax.dot_general(left, right, (dims, ((), ())), preferred_element_type=F32)


def skew(value, step):
    rows, width = value.shape
    row = lax.broadcasted_iota(jnp.int32, value.shape, 0)
    bit = 1
    while bit < rows:
        moved = pltpu.roll(value, (bit * step) % width, 1)
        value = jnp.where((row & bit) != 0, moved, value)
        bit *= 2
    return value


def group_taps(taps_ref, count):
    group = lax.axis_index("seq") * count // GROUP
    row = lax.broadcasted_iota(jnp.int32, taps_ref.shape, 0)
    return jnp.sum(jnp.where(row == group, taps_ref[...].astype(F32), 0.0), axis=0, keepdims=True)


def slide(line, rows):
    return pltpu.roll(jnp.broadcast_to(line, (rows, line.shape[1])), 0, 1, stride=1, stride_axis=0)


def three(highs, lows, tables, dims=((1,), (0,))):
    high = jnp.concatenate(highs, axis=0)
    low = jnp.concatenate(lows, axis=0)
    return dot(high, tables[0], dims) + (dot(low, tables[0], dims) + dot(high, tables[1], dims))


def channel_rows(ref, first, stride, blocks):
    return ref[pl.ds(first, blocks, stride=stride), :]


def enter_grid(columns, enter_ref, twist_ref):
    blocks, width = columns[0].shape
    side = jnp.concatenate(columns, axis=1)
    grid = dot(enter_ref[...], jnp.concatenate([side, side], axis=0))
    twist_real, twist_imag = twist_ref[0], twist_ref[1]
    highs, lows = [], []
    for n in range(len(columns)):
        real = grid[:blocks, n * width : (n + 1) * width]
        imag = grid[blocks:, n * width : (n + 1) * width]
        high, low = split(
            jnp.concatenate(
                [real * twist_real - imag * twist_imag, real * twist_imag + imag * twist_real], axis=1
            )
        )
        highs.append(high)
        lows.append(low)
    return highs, lows


def correlate(lefts, rights, enter_ref, twist_ref, inner_ref, fine):
    blocks = lefts[0].shape[0]
    width = lefts[0].shape[1] // 2
    twist_real, twist_imag = twist_ref[0], twist_ref[1]
    transposed = ((1,), (1,))
    products = []
    for left, right in zip(lefts, rights):
        left_real, left_imag = left[:, :width], left[:, width:]
        real, imag = right[:, :width], right[:, width:]
        products.append(
            jnp.concatenate(
                [left_real * real + left_imag * imag, left_imag * real - left_real * imag], axis=1
            )
        )
    if fine:
        highs, lows = zip(*[split(product) for product in products])
        backs = three(highs, lows, inner_ref, transposed)
    else:
        high = jnp.concatenate([product.astype(BF16) for product in products], axis=0)
        backs = dot(high, inner_ref[0], transposed)
    reals, imags = [], []
    for n in range(len(lefts)):
        real = backs[n * blocks : (n + 1) * blocks, :width]
        imag = backs[n * blocks : (n + 1) * blocks, width:]
        reals.append(real * twist_real + imag * twist_imag)
        imags.append(imag * twist_real - real * twist_imag)
    grid = jnp.concatenate([jnp.concatenate(reals, axis=1), jnp.concatenate(imags, axis=1)], axis=0)
    leave = enter_ref[...].T
    if fine:
        high, low = split(grid)
        wide = dot(leave, high)
        result = wide[:blocks] + (wide[blocks:] + dot(leave[:blocks], low))
    else:
        result = dot(leave[:blocks], grid.astype(BF16))
    return result * (1.0 / (blocks * width))


def filter_side_kernel(
    got_ref, taps_ref, enter_ref, twist_ref, inner_ref,
    spectrum_ref, raw_ref, square_ref, rows_ref,
):
    blocks, lanes_in, width = got_ref.shape
    count = lanes_in // 3
    lanes_here = 2 * count
    rows_ref[...] = got_ref[:, :lanes_here].astype(F32).reshape(blocks * lanes_here, width)
    ahead = jnp.concatenate([jnp.zeros((1, width), F32), group_taps(taps_ref, count)], axis=1)
    mix_table = slide(ahead, 2 * width)[:, :width].astype(BF16)
    row = lax.broadcasted_iota(jnp.int32, (blocks, width), 0)
    pairs, columns = [], []
    for c in range(count):
        signal = channel_rows(rows_ref, c, lanes_here, blocks)
        before = jnp.where(row == 0, 0.0, pltpu.roll(signal, 1, 0))
        pairs.append(jnp.concatenate([before, signal], axis=1).astype(BF16))
        columns.append(channel_rows(rows_ref, count + c, lanes_here, blocks).astype(BF16))
    mixed = dot(jnp.concatenate(pairs, axis=0), mix_table).astype(BF16)
    columns += [mixed[c * blocks : (c + 1) * blocks] for c in range(count)]
    highs, lows = enter_grid(columns, enter_ref, twist_ref)
    spectra = three(highs, lows, inner_ref)
    spectrum_ref[...] = spectra[: count * blocks]
    lefts = [spectra[c * blocks : (c + 1) * blocks] for c in range(count)]
    rights = [spectra[(count + c) * blocks : (count + c + 1) * blocks] for c in range(count)]
    result = correlate(lefts, rights, enter_ref, twist_ref, inner_ref, False)
    squares = jnp.zeros((blocks, width), F32)
    for c in range(count):
        raw = result[:, c * width : (c + 1) * width].astype(BF16)
        raw_ref[c] = raw
        squares = squares + raw.astype(F32) * raw.astype(F32)
    total = jnp.sum(squares, axis=(0, 1), keepdims=True)
    square_ref[...] = jnp.broadcast_to(total[None], square_ref.shape)


def signal_side_kernel(
    got_ref, spectrum_ref, raw_ref, taps_ref, skip_ref, enter_ref, twist_ref, inner_ref,
    out_ref, short_ref, rows_ref, made_ref,
):
    blocks, pairs_out, _, width = out_ref.shape
    count = pairs_out - 1
    lanes_in = 3 * count
    rows_ref[...] = got_ref[...].astype(F32).reshape(blocks * lanes_in, width)
    behind = jnp.concatenate([group_taps(taps_ref, count), jnp.zeros((1, width), F32)], axis=1)
    unmix_table = slide(behind, width).astype(BF16)
    row = lax.broadcasted_iota(jnp.int32, (blocks, width), 0)
    columns = [channel_rows(rows_ref, 2 * count + c, lanes_in, blocks).astype(BF16) for c in range(count)]
    highs, lows = enter_grid(columns, enter_ref, twist_ref)
    spectra = three(highs, lows, inner_ref)
    lefts = [spectrum_ref[c * blocks : (c + 1) * blocks, :] for c in range(count)]
    rights = [spectra[c * blocks : (c + 1) * blocks] for c in range(count)]
    result = correlate(lefts, rights, enter_ref, twist_ref, inner_ref, True)
    first = lax.axis_index("seq") * count
    pairs, grads, signals = [], [], []
    for c in range(count):
        upstream = channel_rows(rows_ref, count + c, lanes_in, blocks)
        grad = (skip_ref[first + c] * upstream + result[:, c * width : (c + 1) * width]).astype(BF16)
        after = jnp.where(row == blocks - 1, 0.0, pltpu.roll(grad.astype(F32), blocks - 1, 0))
        pairs.append(jnp.concatenate([grad, after.astype(BF16)], axis=1))
        grads.append(grad)
        signal = channel_rows(rows_ref, c, lanes_in, blocks)
        before = jnp.where(row == 0, 0.0, pltpu.roll(signal, 1, 0))
        signals.append(jnp.concatenate([before, signal], axis=1).astype(BF16))
    made = dot(jnp.concatenate(pairs, axis=0), unmix_table, ((1,), (1,)))
    for c in range(count):
        made_ref[pl.ds(c, blocks, stride=2 * count), :] = raw_ref[c].astype(F32)
        made_ref[pl.ds(count + c, blocks, stride=2 * count), :] = made[c * blocks : (c + 1) * blocks]
    out_ref[:, :count] = made_ref[...].reshape(blocks, count, 2, width).astype(BF16)
    out_ref[:, count:] = jnp.zeros((blocks, 1, 2, width), BF16)
    table = dot(jnp.concatenate(grads, axis=0), jnp.concatenate(signals, axis=0), ((0,), (0,)))
    turned = table.T
    source = lax.broadcasted_iota(jnp.int32, turned.shape, 0)
    place = lax.broadcasted_iota(jnp.int32, turned.shape, 1)
    inside = jnp.logical_and(place < source, source <= place + width)
    lined = skew(jnp.where(inside, turned, 0.0), -1)
    short_ref[...] = jnp.broadcast_to(jnp.sum(lined, axis=0, keepdims=True), short_ref.shape)


def filter_side(got, taps, tables, slabs):
    blocks, lanes_in, width = got.shape
    count = lanes_in // 3
    vmem = pl.BlockSpec(memory_space=pltpu.VMEM)
    return pl.pallas_call(
        filter_side_kernel,
        out_shape=(
            jax.ShapeDtypeStruct((count * blocks, 2 * width), F32),
            jax.ShapeDtypeStruct((count, blocks, width), BF16),
            jax.ShapeDtypeStruct((slabs, 8, width), F32),
        ),
        in_specs=[vmem] * 5,
        out_specs=(vmem,) * 3,
        scratch_shapes=[
            pltpu.VMEM((blocks * 2 * count, width), F32),
        ],
        compiler_params=pltpu.CompilerParams(vmem_limit_bytes=40 * 2**20),
        cost_estimate=pl.CostEstimate(flops=3 * 10**9, bytes_accessed=6 * 10**6, transcendentals=0),
    )(got, taps, *tables)


def signal_side(got, spectrum, raw, taps, skip, tables):
    blocks, lanes_in, width = got.shape
    count = lanes_in // 3
    vmem = pl.BlockSpec(memory_space=pltpu.VMEM)
    return pl.pallas_call(
        signal_side_kernel,
        out_shape=(
            jax.ShapeDtypeStruct((blocks, count + 1, 2, width), BF16),
            jax.ShapeDtypeStruct((8, width), F32),
        ),
        in_specs=[vmem] * 4 + [pl.BlockSpec(memory_space=pltpu.SMEM)] + [vmem] * 3,
        out_specs=(vmem, vmem),
        scratch_shapes=[
            pltpu.VMEM((blocks * lanes_in, width), F32),
            pltpu.VMEM((blocks * 2 * count, width), F32),
        ],
        compiler_params=pltpu.CompilerParams(vmem_limit_bytes=40 * 2**20),
        cost_estimate=pl.CostEstimate(flops=3 * 10**9, bytes_accessed=6 * 10**6, transcendentals=0),
    )(got, spectrum, raw, taps, skip, *tables)


def stamp_kernel(message_ref, short_ref, squares_ref, out_ref, extra_ref, sem):
    del message_ref
    blocks, _, width = extra_ref.shape
    short = short_ref[:1, :]
    short_high = short.astype(BF16).astype(F32)
    square = jnp.sum(squares_ref[...], axis=0)[:1, :]
    square_high = square.astype(BF16).astype(F32)
    lane = lax.broadcasted_iota(jnp.int32, (1, width), 1)
    rest = jnp.where(lane == 0, square_high, jnp.where(lane == 1, square - square_high, short - short_high))
    both = jnp.concatenate([short_high, rest], axis=0)
    extra_ref[...] = jnp.broadcast_to(both[None], extra_ref.shape).astype(BF16)
    copy = pltpu.make_async_copy(extra_ref, out_ref.at[:, out_ref.shape[1] - 1], sem)
    copy.start()
    copy.wait()


def stamp(message, short, squares):
    blocks, _, _, width = message.shape
    vmem = pl.BlockSpec(memory_space=pltpu.VMEM)
    hbm = pl.BlockSpec(memory_space=pl.ANY)
    return pl.pallas_call(
        stamp_kernel,
        out_shape=jax.ShapeDtypeStruct(message.shape, BF16),
        in_specs=[hbm, vmem, vmem],
        out_specs=hbm,
        input_output_aliases={0: 0},
        scratch_shapes=[pltpu.VMEM((blocks, 2, width), BF16), pltpu.SemaphoreType.DMA],
        compiler_params=pltpu.CompilerParams(vmem_limit_bytes=8 * 2**20),
    )(message, short, squares)


def pack_kernel(first_ref, second_ref, third_ref, out_ref, held_ref, sems):
    owners, lanes_out, rows = out_ref.shape
    count = lanes_out // 3
    copies = [
        pltpu.make_async_copy(ref, held_ref.at[i], sems.at[i])
        for i, ref in enumerate((first_ref, second_ref, third_ref))
    ]
    for copy in copies:
        copy.start()
    for i, copy in enumerate(copies):
        copy.wait()
        out_ref[:, i * count : (i + 1) * count, :] = held_ref[i].T.reshape(owners, count, rows)


def pack(first, second, third, owners):
    rows, channels = first.shape
    hbm = pl.BlockSpec(memory_space=pl.ANY)
    first, second, third = [pltpu.with_memory_space_constraint(x, pltpu.HBM) for x in (first, second, third)]
    return pl.pallas_call(
        pack_kernel,
        out_shape=jax.ShapeDtypeStruct((owners, 3 * channels // owners, rows), BF16),
        in_specs=[hbm] * 3,
        out_specs=pl.BlockSpec(memory_space=pltpu.VMEM),
        scratch_shapes=[pltpu.VMEM((3, rows, channels), BF16), pltpu.SemaphoreType.DMA((3,))],
        compiler_params=pltpu.CompilerParams(vmem_limit_bytes=16 * 2**20),
        cost_estimate=pl.CostEstimate(flops=10**6, bytes_accessed=6 * rows * channels * 2, transcendentals=0),
    )(first, second, third)


def finish_kernel(entries, scale, back_ref, signal_ref, filter_ref, short_ref):
    parts, pairs, _, rows = back_ref.shape
    half = (pairs - 1) // 2
    channels = signal_ref.shape[1]
    groups = short_ref.shape[0]
    extra = back_ref[:, pairs - 1].astype(F32)
    high, low = extra[:, 0], extra[:, 1]
    lane = lax.broadcasted_iota(jnp.int32, low.shape, 1)
    short = high + jnp.where(lane < 2, 0.0, low)
    short_ref[...] = jnp.sum(short.reshape(groups, parts // groups, rows), axis=1) * scale
    squares = jnp.sum(jnp.where(lane < 2, low, 0.0), axis=(0, 1), keepdims=True)
    divisor = jnp.maximum(1.0, jnp.sqrt(squares * (1.0 / entries)))
    signal_ref[...] = back_ref[:, half : 2 * half].astype(F32).reshape(channels, rows).T.astype(BF16)
    raw = back_ref[:, :half].astype(F32).reshape(channels, rows)
    filter_ref[...] = (raw / divisor).T.astype(BF16)


def finish(back, channels, groups, entries, scale):
    rows = back.shape[3]
    vmem = pl.BlockSpec(memory_space=pltpu.VMEM)
    return pl.pallas_call(
        lambda *refs: finish_kernel(entries, scale, *refs),
        out_shape=(
            jax.ShapeDtypeStruct((rows, channels), BF16),
            jax.ShapeDtypeStruct((rows, channels), BF16),
            jax.ShapeDtypeStruct((groups, rows), F32),
        ),
        in_specs=[vmem],
        out_specs=(vmem, vmem, vmem),
        compiler_params=pltpu.CompilerParams(vmem_limit_bytes=16 * 2**20),
    )(back)


def on_device(signal, upstream, long_filter, short_filter, skip_gain):
    rows, channels = signal.shape
    parts = lax.axis_size("seq")
    slabs = lax.axis_size("ch")
    count = channels // parts
    groups = short_filter.shape[1]
    tables = [jnp.asarray(table) for table in dft_tables(parts, rows)]

    got = lax.all_to_all(pack(signal, upstream, long_filter, parts), "seq", 0, 0, tiled=True)
    taps = short_filter.T
    spectrum, raw, squares = filter_side(got, taps, tables, slabs)
    squares = lax.all_to_all(squares, "ch", 0, 0, tiled=True)
    message, short = signal_side(got, spectrum, raw, taps, skip_gain, tables)
    back = lax.all_to_all(stamp(message, short, squares), "seq", 0, 0, tiled=True)
    entries = float(rows * parts * channels * slabs)
    scale = 1.0 / math.sqrt(GROUP * rows * parts)
    grad_signal, grad_long, short = finish(back, channels, groups, entries, scale)
    return (grad_signal, grad_long, short.T)


def solution(mesh):
    placed = (P("seq", "ch"), P("seq", "ch"), P("seq", "ch"), P(None, "ch"), P("ch"))
    return jax.shard_map(
        on_device,
        mesh=mesh,
        in_specs=placed,
        out_specs=(P("seq", "ch"), P("seq", "ch"), P(None, "ch")),
        check_vma=False,
    )
```

```python
import math

import jax
import jax.numpy as jnp
import numpy as np
from jax import lax
from jax.experimental import pallas as pl
from jax.experimental.pallas import tpu as pltpu
from jax.sharding import PartitionSpec as P

GROUP = 16
F32 = jnp.float32
BF16 = jnp.bfloat16


def split_table(table):
    high = table.astype(BF16)
    low = (table - high.astype(np.float64)).astype(BF16)
    return high, low


def dft_tables(blocks, width):
    total = 2 * blocks * width
    k1 = np.arange(blocks)[:, None] + 0.5
    b = np.arange(blocks)[None, :]
    p = np.arange(width)[None, :]
    angle = 2.0 * np.pi * k1 * b / (2 * blocks)
    enter = np.concatenate([np.cos(angle), -np.sin(angle)], axis=0)
    enter_high, enter_low = split_table(enter)
    enter_both = np.concatenate([enter_high, enter_low], axis=1)
    twist_angle = 2.0 * np.pi * k1 * p / total
    twist = np.stack([np.cos(twist_angle), -np.sin(twist_angle)]).astype(np.float32)
    inner_angle = 2.0 * np.pi * np.arange(width)[:, None] * p / width
    cosine, sine = np.cos(inner_angle), np.sin(inner_angle)
    inner = np.block([[cosine, -sine], [sine, cosine]])
    return enter_both, twist, np.stack(split_table(inner))


def split(value):
    high = value.astype(BF16)
    return high, (value - high.astype(F32)).astype(BF16)


def dot(left, right, dims=((1,), (0,))):
    return lax.dot_general(left, right, (dims, ((), ())), preferred_element_type=F32)


def skew(value, step):
    rows, width = value.shape
    row = lax.broadcasted_iota(jnp.int32, value.shape, 0)
    bit = 1
    while bit < rows:
        moved = pltpu.roll(value, (bit * step) % width, 1)
        value = jnp.where((row & bit) != 0, moved, value)
        bit *= 2
    return value


def group_taps(taps_ref, count):
    group = lax.axis_index("seq") * count // GROUP
    row = lax.broadcasted_iota(jnp.int32, taps_ref.shape, 0)
    return jnp.sum(jnp.where(row == group, taps_ref[...].astype(F32), 0.0), axis=0, keepdims=True)


def slide(line, rows):
    return pltpu.roll(jnp.broadcast_to(line, (rows, line.shape[1])), 0, 1, stride=1, stride_axis=0)


def three(highs, lows, tables, dims=((1,), (0,))):
    high = jnp.concatenate(highs, axis=0)
    low = jnp.concatenate(lows, axis=0)
    return dot(high, tables[0], dims) + (dot(low, tables[0], dims) + dot(high, tables[1], dims))


def channel_rows(ref, first, stride, blocks):
    return ref[pl.ds(first, blocks, stride=stride), :]


def enter_grid(columns, enter_ref, twist_ref):
    blocks, width = columns[0].shape
    side = jnp.concatenate(columns, axis=1)
    grid = dot(enter_ref[...], jnp.concatenate([side, side], axis=0))
    twist_real, twist_imag = twist_ref[0], twist_ref[1]
    highs, lows = [], []
    for n in range(len(columns)):
        real = grid[:blocks, n * width : (n + 1) * width]
        imag = grid[blocks:, n * width : (n + 1) * width]
        high, low = split(
            jnp.concatenate(
                [real * twist_real - imag * twist_imag, real * twist_imag + imag * twist_real], axis=1
            )
        )
        highs.append(high)
        lows.append(low)
    return highs, lows


def correlate(lefts, rights, enter_ref, twist_ref, inner_ref, fine):
    blocks = lefts[0].shape[0]
    width = lefts[0].shape[1] // 2
    twist_real, twist_imag = twist_ref[0], twist_ref[1]
    transposed = ((1,), (1,))
    products = []
    for left, right in zip(lefts, rights):
        left_real, left_imag = left[:, :width], left[:, width:]
        real, imag = right[:, :width], right[:, width:]
        products.append(
            jnp.concatenate(
                [left_real * real + left_imag * imag, left_imag * real - left_real * imag], axis=1
            )
        )
    if fine:
        highs, lows = zip(*[split(product) for product in products])
        backs = three(highs, lows, inner_ref, transposed)
    else:
        high = jnp.concatenate([product.astype(BF16) for product in products], axis=0)
        backs = dot(high, inner_ref[0], transposed)
    reals, imags = [], []
    for n in range(len(lefts)):
        real = backs[n * blocks : (n + 1) * blocks, :width]
        imag = backs[n * blocks : (n + 1) * blocks, width:]
        reals.append(real * twist_real + imag * twist_imag)
        imags.append(imag * twist_real - real * twist_imag)
    grid = jnp.concatenate([jnp.concatenate(reals, axis=1), jnp.concatenate(imags, axis=1)], axis=0)
    leave = enter_ref[...].T
    if fine:
        high, low = split(grid)
        wide = dot(leave, high)
        result = wide[:blocks] + (wide[blocks:] + dot(leave[:blocks], low))
    else:
        result = dot(leave[:blocks], grid.astype(BF16))
    return result * (1.0 / (blocks * width))


def filter_side_kernel(
    got_ref, taps_ref, enter_ref, twist_ref, inner_ref,
    spectrum_ref, raw_ref, square_ref, rows_ref,
):
    blocks, lanes_in, width = got_ref.shape
    count = lanes_in // 3
    lanes_here = 2 * count
    rows_ref[...] = got_ref[:, :lanes_here].astype(F32).reshape(blocks * lanes_here, width)
    ahead = jnp.concatenate([jnp.zeros((1, width), F32), group_taps(taps_ref, count)], axis=1)
    mix_table = slide(ahead, 2 * width)[:, :width].astype(BF16)
    row = lax.broadcasted_iota(jnp.int32, (blocks, width), 0)
    pairs, columns = [], []
    for c in range(count):
        signal = channel_rows(rows_ref, c, lanes_here, blocks)
        before = jnp.where(row == 0, 0.0, pltpu.roll(signal, 1, 0))
        pairs.append(jnp.concatenate([before, signal], axis=1).astype(BF16))
        columns.append(channel_rows(rows_ref, count + c, lanes_here, blocks).astype(BF16))
    mixed = dot(jnp.concatenate(pairs, axis=0), mix_table).astype(BF16)
    highs, lows = enter_grid(columns, enter_ref, twist_ref)
    upstreams = three(highs, lows, inner_ref)
    spectrum_ref[...] = upstreams
    columns = [mixed[c * blocks : (c + 1) * blocks] for c in range(count)]
    highs, lows = enter_grid(columns, enter_ref, twist_ref)
    mixeds = three(highs, lows, inner_ref)
    lefts = [upstreams[c * blocks : (c + 1) * blocks] for c in range(count)]
    rights = [mixeds[c * blocks : (c + 1) * blocks] for c in range(count)]
    result = correlate(lefts, rights, enter_ref, twist_ref, inner_ref, False)
    squares = jnp.zeros((blocks, width), F32)
    for c in range(count):
        raw = result[:, c * width : (c + 1) * width].astype(BF16)
        raw_ref[c] = raw
        squares = squares + raw.astype(F32) * raw.astype(F32)
    total = jnp.sum(squares, axis=(0, 1), keepdims=True)
    square_ref[...] = jnp.broadcast_to(total[None], square_ref.shape)


def signal_side_kernel(
    got_ref, spectrum_ref, raw_ref, taps_ref, skip_ref, enter_ref, twist_ref, inner_ref,
    out_ref, short_ref, rows_ref, made_ref,
):
    blocks, pairs_out, _, width = out_ref.shape
    count = pairs_out - 1
    lanes_in = 3 * count
    rows_ref[...] = got_ref[...].astype(F32).reshape(blocks * lanes_in, width)
    behind = jnp.concatenate([group_taps(taps_ref, count), jnp.zeros((1, width), F32)], axis=1)
    unmix_table = slide(behind, width).astype(BF16)
    row = lax.broadcasted_iota(jnp.int32, (blocks, width), 0)
    columns = [channel_rows(rows_ref, 2 * count + c, lanes_in, blocks).astype(BF16) for c in range(count)]
    highs, lows = enter_grid(columns, enter_ref, twist_ref)
    spectra = three(highs, lows, inner_ref)
    lefts = [spectrum_ref[c * blocks : (c + 1) * blocks, :] for c in range(count)]
    rights = [spectra[c * blocks : (c + 1) * blocks] for c in range(count)]
    result = correlate(lefts, rights, enter_ref, twist_ref, inner_ref, True)
    first = lax.axis_index("seq") * count
    pairs, grads, signals = [], [], []
    for c in range(count):
        upstream = channel_rows(rows_ref, count + c, lanes_in, blocks)
        grad = (skip_ref[first + c] * upstream + result[:, c * width : (c + 1) * width]).astype(BF16)
        after = jnp.where(row == blocks - 1, 0.0, pltpu.roll(grad.astype(F32), blocks - 1, 0))
        pairs.append(jnp.concatenate([grad, after.astype(BF16)], axis=1))
        grads.append(grad)
        signal = channel_rows(rows_ref, c, lanes_in, blocks)
        before = jnp.where(row == 0, 0.0, pltpu.roll(signal, 1, 0))
        signals.append(jnp.concatenate([before, signal], axis=1).astype(BF16))
    made = dot(jnp.concatenate(pairs, axis=0), unmix_table, ((1,), (1,)))
    for c in range(count):
        made_ref[pl.ds(c, blocks, stride=2 * count), :] = raw_ref[c].astype(F32)
        made_ref[pl.ds(count + c, blocks, stride=2 * count), :] = made[c * blocks : (c + 1) * blocks]
    out_ref[:, :count] = made_ref[...].reshape(blocks, count, 2, width).astype(BF16)
    out_ref[:, count:] = jnp.zeros((blocks, 1, 2, width), BF16)
    table = dot(jnp.concatenate(grads, axis=0), jnp.concatenate(signals, axis=0), ((0,), (0,)))
    turned = table.T
    source = lax.broadcasted_iota(jnp.int32, turned.shape, 0)
    place = lax.broadcasted_iota(jnp.int32, turned.shape, 1)
    inside = jnp.logical_and(place < source, source <= place + width)
    lined = skew(jnp.where(inside, turned, 0.0), -1)
    short_ref[...] = jnp.broadcast_to(jnp.sum(lined, axis=0, keepdims=True), short_ref.shape)


def filter_side(got, taps, tables, slabs):
    blocks, lanes_in, width = got.shape
    count = lanes_in // 3
    vmem = pl.BlockSpec(memory_space=pltpu.VMEM)
    return pl.pallas_call(
        filter_side_kernel,
        out_shape=(
            jax.ShapeDtypeStruct((count * blocks, 2 * width), F32),
            jax.ShapeDtypeStruct((count, blocks, width), BF16),
            jax.ShapeDtypeStruct((slabs, 8, width), F32),
        ),
        in_specs=[vmem] * 5,
        out_specs=(vmem,) * 3,
        scratch_shapes=[
            pltpu.VMEM((blocks * 2 * count, width), F32),
        ],
        compiler_params=pltpu.CompilerParams(vmem_limit_bytes=40 * 2**20),
        cost_estimate=pl.CostEstimate(flops=3 * 10**9, bytes_accessed=6 * 10**6, transcendentals=0),
    )(got, taps, *tables)


def signal_side(got, spectrum, raw, taps, skip, tables):
    blocks, lanes_in, width = got.shape
    count = lanes_in // 3
    vmem = pl.BlockSpec(memory_space=pltpu.VMEM)
    return pl.pallas_call(
        signal_side_kernel,
        out_shape=(
            jax.ShapeDtypeStruct((blocks, count + 1, 2, width), BF16),
            jax.ShapeDtypeStruct((8, width), F32),
        ),
        in_specs=[vmem] * 4 + [pl.BlockSpec(memory_space=pltpu.SMEM)] + [vmem] * 3,
        out_specs=(vmem, vmem),
        scratch_shapes=[
            pltpu.VMEM((blocks * lanes_in, width), F32),
            pltpu.VMEM((blocks * 2 * count, width), F32),
        ],
        compiler_params=pltpu.CompilerParams(vmem_limit_bytes=40 * 2**20),
        cost_estimate=pl.CostEstimate(flops=3 * 10**9, bytes_accessed=6 * 10**6, transcendentals=0),
    )(got, spectrum, raw, taps, skip, *tables)


def stamp_kernel(message_ref, short_ref, squares_ref, out_ref, extra_ref, sem):
    del message_ref
    blocks, _, width = extra_ref.shape
    short = short_ref[:1, :]
    short_high = short.astype(BF16).astype(F32)
    square = jnp.sum(squares_ref[...], axis=0)[:1, :]
    square_high = square.astype(BF16).astype(F32)
    lane = lax.broadcasted_iota(jnp.int32, (1, width), 1)
    rest = jnp.where(lane == 0, square_high, jnp.where(lane == 1, square - square_high, short - short_high))
    both = jnp.concatenate([short_high, rest], axis=0)
    extra_ref[...] = jnp.broadcast_to(both[None], extra_ref.shape).astype(BF16)
    copy = pltpu.make_async_copy(extra_ref, out_ref.at[:, out_ref.shape[1] - 1], sem)
    copy.start()
    copy.wait()


def stamp(message, short, squares):
    blocks, _, _, width = message.shape
    vmem = pl.BlockSpec(memory_space=pltpu.VMEM)
    hbm = pl.BlockSpec(memory_space=pl.ANY)
    return pl.pallas_call(
        stamp_kernel,
        out_shape=jax.ShapeDtypeStruct(message.shape, BF16),
        in_specs=[hbm, vmem, vmem],
        out_specs=hbm,
        input_output_aliases={0: 0},
        scratch_shapes=[pltpu.VMEM((blocks, 2, width), BF16), pltpu.SemaphoreType.DMA],
        compiler_params=pltpu.CompilerParams(vmem_limit_bytes=8 * 2**20),
    )(message, short, squares)


def pack_kernel(first_ref, second_ref, third_ref, out_ref, held_ref, sems):
    owners, lanes_out, rows = out_ref.shape
    count = lanes_out // 3
    copies = [
        pltpu.make_async_copy(ref, held_ref.at[i], sems.at[i])
        for i, ref in enumerate((first_ref, second_ref, third_ref))
    ]
    for copy in copies:
        copy.start()
    for i, copy in enumerate(copies):
        copy.wait()
        out_ref[:, i * count : (i + 1) * count, :] = held_ref[i].T.reshape(owners, count, rows)


def pack(first, second, third, owners):
    rows, channels = first.shape
    hbm = pl.BlockSpec(memory_space=pl.ANY)
    first, second, third = [pltpu.with_memory_space_constraint(x, pltpu.HBM) for x in (first, second, third)]
    return pl.pallas_call(
        pack_kernel,
        out_shape=jax.ShapeDtypeStruct((owners, 3 * channels // owners, rows), BF16),
        in_specs=[hbm] * 3,
        out_specs=pl.BlockSpec(memory_space=pltpu.VMEM),
        scratch_shapes=[pltpu.VMEM((3, rows, channels), BF16), pltpu.SemaphoreType.DMA((3,))],
        compiler_params=pltpu.CompilerParams(vmem_limit_bytes=16 * 2**20),
        cost_estimate=pl.CostEstimate(flops=10**6, bytes_accessed=6 * rows * channels * 2, transcendentals=0),
    )(first, second, third)


def finish_kernel(entries, scale, back_ref, signal_ref, filter_ref, short_ref):
    parts, pairs, _, rows = back_ref.shape
    half = (pairs - 1) // 2
    channels = signal_ref.shape[1]
    groups = short_ref.shape[0]
    extra = back_ref[:, pairs - 1].astype(F32)
    high, low = extra[:, 0], extra[:, 1]
    lane = lax.broadcasted_iota(jnp.int32, low.shape, 1)
    short = high + jnp.where(lane < 2, 0.0, low)
    short_ref[...] = jnp.sum(short.reshape(groups, parts // groups, rows), axis=1) * scale
    squares = jnp.sum(jnp.where(lane < 2, low, 0.0), axis=(0, 1), keepdims=True)
    divisor = jnp.maximum(1.0, jnp.sqrt(squares * (1.0 / entries)))
    signal_ref[...] = back_ref[:, half : 2 * half].astype(F32).reshape(channels, rows).T.astype(BF16)
    raw = back_ref[:, :half].astype(F32).reshape(channels, rows)
    filter_ref[...] = (raw / divisor).T.astype(BF16)


def finish(back, channels, groups, entries, scale):
    rows = back.shape[3]
    vmem = pl.BlockSpec(memory_space=pltpu.VMEM)
    return pl.pallas_call(
        lambda *refs: finish_kernel(entries, scale, *refs),
        out_shape=(
            jax.ShapeDtypeStruct((rows, channels), BF16),
            jax.ShapeDtypeStruct((rows, channels), BF16),
            jax.ShapeDtypeStruct((groups, rows), F32),
        ),
        in_specs=[vmem],
        out_specs=(vmem, vmem, vmem),
        compiler_params=pltpu.CompilerParams(vmem_limit_bytes=16 * 2**20),
    )(back)


def on_device(signal, upstream, long_filter, short_filter, skip_gain):
    rows, channels = signal.shape
    parts = lax.axis_size("seq")
    slabs = lax.axis_size("ch")
    count = channels // parts
    groups = short_filter.shape[1]
    tables = [jnp.asarray(table) for table in dft_tables(parts, rows)]

    got = lax.all_to_all(pack(signal, upstream, long_filter, parts), "seq", 0, 0, tiled=True)
    taps = short_filter.T
    spectrum, raw, squares = filter_side(got, taps, tables, slabs)
    squares = lax.all_to_all(squares, "ch", 0, 0, tiled=True)
    message, short = signal_side(got, spectrum, raw, taps, skip_gain, tables)
    back = lax.all_to_all(stamp(message, short, squares), "seq", 0, 0, tiled=True)
    entries = float(rows * parts * channels * slabs)
    scale = 1.0 / math.sqrt(GROUP * rows * parts)
    grad_signal, grad_long, short = finish(back, channels, groups, entries, scale)
    return (grad_signal, grad_long, short.T)


def solution(mesh):
    placed = (P("seq", "ch"), P("seq", "ch"), P("seq", "ch"), P(None, "ch"), P("ch"))
    return jax.shard_map(
        on_device,
        mesh=mesh,
        in_specs=placed,
        out_specs=(P("seq", "ch"), P("seq", "ch"), P(None, "ch")),
        check_vma=False,
    )
```

```python
import math

import jax
import jax.numpy as jnp
import numpy as np
from jax import lax
from jax.experimental import pallas as pl
from jax.experimental.pallas import tpu as pltpu
from jax.sharding import PartitionSpec as P

GROUP = 16
F32 = jnp.float32
BF16 = jnp.bfloat16


def split_table(table):
    high = table.astype(BF16)
    low = (table - high.astype(np.float64)).astype(BF16)
    return high, low


def dft_tables(blocks, width):
    total = 2 * blocks * width
    k1 = np.arange(blocks)[:, None] + 0.5
    b = np.arange(blocks)[None, :]
    p = np.arange(width)[None, :]
    angle = 2.0 * np.pi * k1 * b / (2 * blocks)
    enter = np.concatenate([np.cos(angle), -np.sin(angle)], axis=0)
    enter_high, enter_low = split_table(enter)
    enter_both = np.concatenate([enter_high, enter_low], axis=1)
    twist_angle = 2.0 * np.pi * k1 * p / total
    twist = np.stack([np.cos(twist_angle), -np.sin(twist_angle)]).astype(np.float32)
    inner_angle = 2.0 * np.pi * np.arange(width)[:, None] * p / width
    cosine, sine = np.cos(inner_angle), np.sin(inner_angle)
    inner = np.block([[cosine, -sine], [sine, cosine]])
    return enter_both, twist, np.stack(split_table(inner))


def split(value):
    high = value.astype(BF16)
    return high, (value - high.astype(F32)).astype(BF16)


def dot(left, right, dims=((1,), (0,))):
    return lax.dot_general(left, right, (dims, ((), ())), preferred_element_type=F32)


def skew(value, step):
    rows, width = value.shape
    row = lax.broadcasted_iota(jnp.int32, value.shape, 0)
    bit = 1
    while bit < rows:
        moved = pltpu.roll(value, (bit * step) % width, 1)
        value = jnp.where((row & bit) != 0, moved, value)
        bit *= 2
    return value


def group_taps(taps_ref, count):
    group = lax.axis_index("seq") * count // GROUP
    row = lax.broadcasted_iota(jnp.int32, taps_ref.shape, 0)
    return jnp.sum(jnp.where(row == group, taps_ref[...].astype(F32), 0.0), axis=0, keepdims=True)


def slide(line, rows):
    return pltpu.roll(jnp.broadcast_to(line, (rows, line.shape[1])), 0, 1, stride=1, stride_axis=0)


def three(highs, lows, tables, dims=((1,), (0,))):
    high = jnp.concatenate(highs, axis=0)
    low = jnp.concatenate(lows, axis=0)
    return dot(high, tables[0], dims) + (dot(low, tables[0], dims) + dot(high, tables[1], dims))


def channel_rows(ref, first, stride, blocks):
    return ref[pl.ds(first, blocks, stride=stride), :]


def enter_grid(columns, enter_ref, twist_ref):
    blocks, width = columns[0].shape
    side = jnp.concatenate(columns, axis=1)
    grid = dot(enter_ref[...], jnp.concatenate([side, side], axis=0))
    twist_real, twist_imag = twist_ref[0], twist_ref[1]
    highs, lows = [], []
    for n in range(len(columns)):
        real = grid[:blocks, n * width : (n + 1) * width]
        imag = grid[blocks:, n * width : (n + 1) * width]
        high, low = split(
            jnp.concatenate(
                [real * twist_real - imag * twist_imag, real * twist_imag + imag * twist_real], axis=1
            )
        )
        highs.append(high)
        lows.append(low)
    return highs, lows


def correlate(lefts, rights, enter_ref, twist_ref, inner_ref, fine):
    blocks = lefts[0].shape[0]
    width = lefts[0].shape[1] // 2
    twist_real, twist_imag = twist_ref[0], twist_ref[1]
    transposed = ((1,), (1,))
    products = []
    for left, right in zip(lefts, rights):
        left_real, left_imag = left[:, :width], left[:, width:]
        real, imag = right[:, :width], right[:, width:]
        products.append(
            jnp.concatenate(
                [left_real * real + left_imag * imag, left_imag * real - left_real * imag], axis=1
            )
        )
    if fine:
        highs, lows = zip(*[split(product) for product in products])
        backs = three(highs, lows, inner_ref, transposed)
    else:
        high = jnp.concatenate([product.astype(BF16) for product in products], axis=0)
        backs = dot(high, inner_ref[0], transposed)
    reals, imags = [], []
    for n in range(len(lefts)):
        real = backs[n * blocks : (n + 1) * blocks, :width]
        imag = backs[n * blocks : (n + 1) * blocks, width:]
        reals.append(real * twist_real + imag * twist_imag)
        imags.append(imag * twist_real - real * twist_imag)
    grid = jnp.concatenate([jnp.concatenate(reals, axis=1), jnp.concatenate(imags, axis=1)], axis=0)
    leave = enter_ref[...].T
    if fine:
        high, low = split(grid)
        wide = dot(leave, high)
        result = wide[:blocks] + (wide[blocks:] + dot(leave[:blocks], low))
    else:
        result = dot(leave[:blocks], grid.astype(BF16))
    return result * (1.0 / (blocks * width))


def filter_side_kernel(
    got_ref, taps_ref, enter_ref, twist_ref, inner_ref,
    spectrum_ref, raw_ref, square_ref, rows_ref,
):
    blocks, lanes_in, width = got_ref.shape
    count = lanes_in // 3
    lanes_here = 2 * count
    rows_ref[...] = got_ref[:, :lanes_here].astype(F32).reshape(blocks * lanes_here, width)
    ahead = jnp.concatenate([jnp.zeros((1, width), F32), group_taps(taps_ref, count)], axis=1)
    mix_table = slide(ahead, 2 * width)[:, :width].astype(BF16)
    row = lax.broadcasted_iota(jnp.int32, (blocks, width), 0)
    pairs, columns = [], []
    for c in range(count):
        signal = channel_rows(rows_ref, c, lanes_here, blocks)
        before = jnp.where(row == 0, 0.0, pltpu.roll(signal, 1, 0))
        pairs.append(jnp.concatenate([before, signal], axis=1).astype(BF16))
        columns.append(channel_rows(rows_ref, count + c, lanes_here, blocks).astype(BF16))
    mixed = dot(jnp.concatenate(pairs, axis=0), mix_table).astype(BF16)
    highs, lows = enter_grid(columns, enter_ref, twist_ref)
    upstreams = three(highs, lows, inner_ref)
    spectrum_ref[...] = upstreams
    columns = [mixed[c * blocks : (c + 1) * blocks] for c in range(count)]
    highs, lows = enter_grid(columns, enter_ref, twist_ref)
    mixeds = three(highs, lows, inner_ref)
    lefts = [upstreams[c * blocks : (c + 1) * blocks] for c in range(count)]
    rights = [mixeds[c * blocks : (c + 1) * blocks] for c in range(count)]
    result = correlate(lefts, rights, enter_ref, twist_ref, inner_ref, False)
    squares = jnp.zeros((blocks, width), F32)
    for c in range(count):
        raw = result[:, c * width : (c + 1) * width].astype(BF16)
        raw_ref[c] = raw
        squares = squares + raw.astype(F32) * raw.astype(F32)
    total = jnp.sum(squares, axis=(0, 1), keepdims=True)
    square_ref[...] = jnp.broadcast_to(total[None], square_ref.shape)


def signal_side_kernel(
    got_ref, spectrum_ref, raw_ref, taps_ref, skip_ref, enter_ref, twist_ref, inner_ref,
    out_ref, short_ref, rows_ref, made_ref,
):
    blocks, pairs_out, _, width = out_ref.shape
    count = pairs_out - 1
    lanes_in = 3 * count
    rows_ref[...] = got_ref[...].astype(F32).reshape(blocks * lanes_in, width)
    behind = jnp.concatenate([group_taps(taps_ref, count), jnp.zeros((1, width), F32)], axis=1)
    unmix_table = slide(behind, width).astype(BF16)
    row = lax.broadcasted_iota(jnp.int32, (blocks, width), 0)
    columns = [channel_rows(rows_ref, 2 * count + c, lanes_in, blocks).astype(BF16) for c in range(count)]
    highs, lows = enter_grid(columns, enter_ref, twist_ref)
    spectra = three(highs, lows, inner_ref)
    lefts = [spectrum_ref[c * blocks : (c + 1) * blocks, :] for c in range(count)]
    rights = [spectra[c * blocks : (c + 1) * blocks] for c in range(count)]
    result = correlate(lefts, rights, enter_ref, twist_ref, inner_ref, True)
    first = lax.axis_index("seq") * count
    pairs, grads, signals = [], [], []
    for c in range(count):
        upstream = channel_rows(rows_ref, count + c, lanes_in, blocks)
        grad = (skip_ref[first + c] * upstream + result[:, c * width : (c + 1) * width]).astype(BF16)
        after = jnp.where(row == blocks - 1, 0.0, pltpu.roll(grad.astype(F32), blocks - 1, 0))
        pairs.append(jnp.concatenate([grad, after.astype(BF16)], axis=1))
        grads.append(grad)
        signal = channel_rows(rows_ref, c, lanes_in, blocks)
        before = jnp.where(row == 0, 0.0, pltpu.roll(signal, 1, 0))
        signals.append(jnp.concatenate([before, signal], axis=1).astype(BF16))
    made = dot(jnp.concatenate(pairs, axis=0), unmix_table, ((1,), (1,)))
    for c in range(count):
        made_ref[pl.ds(c, blocks, stride=2 * count), :] = raw_ref[c].astype(F32)
        made_ref[pl.ds(count + c, blocks, stride=2 * count), :] = made[c * blocks : (c + 1) * blocks]
    out_ref[:, :count] = made_ref[...].reshape(blocks, count, 2, width).astype(BF16)
    out_ref[:, count:] = jnp.zeros((blocks, 1, 2, width), BF16)
    table = dot(jnp.concatenate(grads, axis=0), jnp.concatenate(signals, axis=0), ((0,), (0,)))
    turned = table.T
    source = lax.broadcasted_iota(jnp.int32, turned.shape, 0)
    place = lax.broadcasted_iota(jnp.int32, turned.shape, 1)
    inside = jnp.logical_and(place < source, source <= place + width)
    lined = skew(jnp.where(inside, turned, 0.0), -1)
    short_ref[...] = jnp.broadcast_to(jnp.sum(lined, axis=0, keepdims=True), short_ref.shape)


def filter_side(got, taps, tables, slabs):
    blocks, lanes_in, width = got.shape
    count = lanes_in // 3
    vmem = pl.BlockSpec(memory_space=pltpu.VMEM)
    return pl.pallas_call(
        filter_side_kernel,
        out_shape=(
            jax.ShapeDtypeStruct((count * blocks, 2 * width), F32),
            jax.ShapeDtypeStruct((count, blocks, width), BF16),
            jax.ShapeDtypeStruct((slabs, 1, width), F32),
        ),
        in_specs=[vmem] * 5,
        out_specs=(vmem,) * 3,
        scratch_shapes=[
            pltpu.VMEM((blocks * 2 * count, width), F32),
        ],
        compiler_params=pltpu.CompilerParams(vmem_limit_bytes=40 * 2**20),
        cost_estimate=pl.CostEstimate(flops=3 * 10**9, bytes_accessed=6 * 10**6, transcendentals=0),
    )(got, taps, *tables)


def signal_side(got, spectrum, raw, taps, skip, tables):
    blocks, lanes_in, width = got.shape
    count = lanes_in // 3
    vmem = pl.BlockSpec(memory_space=pltpu.VMEM)
    return pl.pallas_call(
        signal_side_kernel,
        out_shape=(
            jax.ShapeDtypeStruct((blocks, count + 1, 2, width), BF16),
            jax.ShapeDtypeStruct((8, width), F32),
        ),
        in_specs=[vmem] * 4 + [pl.BlockSpec(memory_space=pltpu.SMEM)] + [vmem] * 3,
        out_specs=(vmem, vmem),
        scratch_shapes=[
            pltpu.VMEM((blocks * lanes_in, width), F32),
            pltpu.VMEM((blocks * 2 * count, width), F32),
        ],
        compiler_params=pltpu.CompilerParams(vmem_limit_bytes=40 * 2**20),
        cost_estimate=pl.CostEstimate(flops=3 * 10**9, bytes_accessed=6 * 10**6, transcendentals=0),
    )(got, spectrum, raw, taps, skip, *tables)


def stamp_kernel(message_ref, short_ref, squares_ref, out_ref, extra_ref, sem):
    del message_ref
    blocks, _, width = extra_ref.shape
    short = short_ref[:1, :]
    short_high = short.astype(BF16).astype(F32)
    square = jnp.sum(squares_ref[...], axis=0)[:1, :]
    square_high = square.astype(BF16).astype(F32)
    lane = lax.broadcasted_iota(jnp.int32, (1, width), 1)
    rest = jnp.where(lane == 0, square_high, jnp.where(lane == 1, square - square_high, short - short_high))
    both = jnp.concatenate([short_high, rest], axis=0)
    extra_ref[...] = jnp.broadcast_to(both[None], extra_ref.shape).astype(BF16)
    copy = pltpu.make_async_copy(extra_ref, out_ref.at[:, out_ref.shape[1] - 1], sem)
    copy.start()
    copy.wait()


def stamp(message, short, squares):
    blocks, _, _, width = message.shape
    vmem = pl.BlockSpec(memory_space=pltpu.VMEM)
    hbm = pl.BlockSpec(memory_space=pl.ANY)
    return pl.pallas_call(
        stamp_kernel,
        out_shape=jax.ShapeDtypeStruct(message.shape, BF16),
        in_specs=[hbm, vmem, vmem],
        out_specs=hbm,
        input_output_aliases={0: 0},
        scratch_shapes=[pltpu.VMEM((blocks, 2, width), BF16), pltpu.SemaphoreType.DMA],
        compiler_params=pltpu.CompilerParams(vmem_limit_bytes=8 * 2**20),
    )(message, short, squares)


def pack_kernel(first_ref, second_ref, third_ref, out_ref, held_ref, sems):
    owners, lanes_out, rows = out_ref.shape
    count = lanes_out // 3
    copies = [
        pltpu.make_async_copy(ref, held_ref.at[i], sems.at[i])
        for i, ref in enumerate((first_ref, second_ref, third_ref))
    ]
    for copy in copies:
        copy.start()
    for i, copy in enumerate(copies):
        copy.wait()
        out_ref[:, i * count : (i + 1) * count, :] = held_ref[i].T.reshape(owners, count, rows)


def pack(first, second, third, owners):
    rows, channels = first.shape
    hbm = pl.BlockSpec(memory_space=pl.ANY)
    first, second, third = [pltpu.with_memory_space_constraint(x, pltpu.HBM) for x in (first, second, third)]
    return pl.pallas_call(
        pack_kernel,
        out_shape=jax.ShapeDtypeStruct((owners, 3 * channels // owners, rows), BF16),
        in_specs=[hbm] * 3,
        out_specs=pl.BlockSpec(memory_space=pltpu.VMEM),
        scratch_shapes=[pltpu.VMEM((3, rows, channels), BF16), pltpu.SemaphoreType.DMA((3,))],
        compiler_params=pltpu.CompilerParams(vmem_limit_bytes=16 * 2**20),
        cost_estimate=pl.CostEstimate(flops=10**6, bytes_accessed=6 * rows * channels * 2, transcendentals=0),
    )(first, second, third)


def finish_kernel(entries, scale, back_ref, signal_ref, filter_ref, short_ref):
    parts, pairs, _, rows = back_ref.shape
    half = (pairs - 1) // 2
    channels = signal_ref.shape[1]
    groups = short_ref.shape[0]
    extra = back_ref[:, pairs - 1].astype(F32)
    high, low = extra[:, 0], extra[:, 1]
    lane = lax.broadcasted_iota(jnp.int32, low.shape, 1)
    short = high + jnp.where(lane < 2, 0.0, low)
    short_ref[...] = jnp.sum(short.reshape(groups, parts // groups, rows), axis=1) * scale
    squares = jnp.sum(jnp.where(lane < 2, low, 0.0), axis=(0, 1), keepdims=True)
    divisor = jnp.maximum(1.0, jnp.sqrt(squares * (1.0 / entries)))
    signal_ref[...] = back_ref[:, half : 2 * half].astype(F32).reshape(channels, rows).T.astype(BF16)
    raw = back_ref[:, :half].astype(F32).reshape(channels, rows)
    filter_ref[...] = (raw / divisor).T.astype(BF16)


def finish(back, channels, groups, entries, scale):
    rows = back.shape[3]
    vmem = pl.BlockSpec(memory_space=pltpu.VMEM)
    return pl.pallas_call(
        lambda *refs: finish_kernel(entries, scale, *refs),
        out_shape=(
            jax.ShapeDtypeStruct((rows, channels), BF16),
            jax.ShapeDtypeStruct((rows, channels), BF16),
            jax.ShapeDtypeStruct((groups, rows), F32),
        ),
        in_specs=[vmem],
        out_specs=(vmem, vmem, vmem),
        compiler_params=pltpu.CompilerParams(vmem_limit_bytes=16 * 2**20),
    )(back)


def on_device(signal, upstream, long_filter, short_filter, skip_gain):
    rows, channels = signal.shape
    parts = lax.axis_size("seq")
    slabs = lax.axis_size("ch")
    count = channels // parts
    groups = short_filter.shape[1]
    tables = [jnp.asarray(table) for table in dft_tables(parts, rows)]

    got = lax.all_to_all(pack(signal, upstream, long_filter, parts), "seq", 0, 0, tiled=True)
    taps = short_filter.T
    spectrum, raw, squares = filter_side(got, taps, tables, slabs)
    squares = lax.all_to_all(squares, "ch", 0, 0, tiled=True)
    message, short = signal_side(got, spectrum, raw, taps, skip_gain, tables)
    back = lax.all_to_all(stamp(message, short, squares), "seq", 0, 0, tiled=True)
    entries = float(rows * parts * channels * slabs)
    scale = 1.0 / math.sqrt(GROUP * rows * parts)
    grad_signal, grad_long, short = finish(back, channels, groups, entries, scale)
    return (grad_signal, grad_long, short.T)


def solution(mesh):
    placed = (P("seq", "ch"), P("seq", "ch"), P("seq", "ch"), P(None, "ch"), P("ch"))
    return jax.shard_map(
        on_device,
        mesh=mesh,
        in_specs=placed,
        out_specs=(P("seq", "ch"), P("seq", "ch"), P(None, "ch")),
        check_vma=False,
    )
```

```python
import math

import jax
import jax.numpy as jnp
import numpy as np
from jax import lax
from jax.experimental import pallas as pl
from jax.experimental.pallas import tpu as pltpu
from jax.sharding import PartitionSpec as P

GROUP = 16
F32 = jnp.float32
BF16 = jnp.bfloat16


def split_table(table):
    high = table.astype(BF16)
    low = (table - high.astype(np.float64)).astype(BF16)
    return high, low


def dft_tables(blocks, width):
    total = 2 * blocks * width
    k1 = np.arange(blocks)[:, None] + 0.5
    b = np.arange(blocks)[None, :]
    p = np.arange(width)[None, :]
    angle = 2.0 * np.pi * k1 * b / (2 * blocks)
    enter = np.concatenate([np.cos(angle), -np.sin(angle)], axis=0)
    enter_high, enter_low = split_table(enter)
    enter_both = np.concatenate([enter_high, enter_low], axis=1)
    twist_angle = 2.0 * np.pi * k1 * p / total
    twist = np.stack([np.cos(twist_angle), -np.sin(twist_angle)]).astype(np.float32)
    inner_angle = 2.0 * np.pi * np.arange(width)[:, None] * p / width
    cosine, sine = np.cos(inner_angle), np.sin(inner_angle)
    inner = np.block([[cosine, -sine], [sine, cosine]])
    return enter_both, twist, np.stack(split_table(inner))


def split(value):
    high = value.astype(BF16)
    return high, (value - high.astype(F32)).astype(BF16)


def dot(left, right, dims=((1,), (0,))):
    return lax.dot_general(left, right, (dims, ((), ())), preferred_element_type=F32)


def skew(value, step):
    rows, width = value.shape
    row = lax.broadcasted_iota(jnp.int32, value.shape, 0)
    bit = 1
    while bit < rows:
        moved = pltpu.roll(value, (bit * step) % width, 1)
        value = jnp.where((row & bit) != 0, moved, value)
        bit *= 2
    return value


def group_taps(taps_ref, count):
    group = lax.axis_index("seq") * count // GROUP
    row = lax.broadcasted_iota(jnp.int32, taps_ref.shape, 0)
    return jnp.sum(jnp.where(row == group, taps_ref[...].astype(F32), 0.0), axis=0, keepdims=True)


def slide(line, rows):
    return pltpu.roll(jnp.broadcast_to(line, (rows, line.shape[1])), 0, 1, stride=1, stride_axis=0)


def three(highs, lows, tables, dims=((1,), (0,))):
    high = jnp.concatenate(highs, axis=0)
    low = jnp.concatenate(lows, axis=0)
    return dot(high, tables[0], dims) + (dot(low, tables[0], dims) + dot(high, tables[1], dims))


def channel_rows(ref, first, stride, blocks):
    return ref[pl.ds(first, blocks, stride=stride), :]


def enter_grid(columns, enter_ref, twist_ref):
    blocks, width = columns[0].shape
    side = jnp.concatenate(columns, axis=1)
    grid = dot(enter_ref[...], jnp.concatenate([side, side], axis=0))
    twist_real, twist_imag = twist_ref[0], twist_ref[1]
    highs, lows = [], []
    for n in range(len(columns)):
        real = grid[:blocks, n * width : (n + 1) * width]
        imag = grid[blocks:, n * width : (n + 1) * width]
        high, low = split(
            jnp.concatenate(
                [real * twist_real - imag * twist_imag, real * twist_imag + imag * twist_real], axis=1
            )
        )
        highs.append(high)
        lows.append(low)
    return highs, lows


def correlate(lefts, rights, enter_ref, twist_ref, inner_ref, fine):
    blocks = lefts[0].shape[0]
    width = lefts[0].shape[1] // 2
    twist_real, twist_imag = twist_ref[0], twist_ref[1]
    transposed = ((1,), (1,))
    products = []
    for left, right in zip(lefts, rights):
        left_real, left_imag = left[:, :width], left[:, width:]
        real, imag = right[:, :width], right[:, width:]
        products.append(
            jnp.concatenate(
                [left_real * real + left_imag * imag, left_imag * real - left_real * imag], axis=1
            )
        )
    if fine:
        highs, lows = zip(*[split(product) for product in products])
        backs = three(highs, lows, inner_ref, transposed)
    else:
        high = jnp.concatenate([product.astype(BF16) for product in products], axis=0)
        backs = dot(high, inner_ref[0], transposed)
    reals, imags = [], []
    for n in range(len(lefts)):
        real = backs[n * blocks : (n + 1) * blocks, :width]
        imag = backs[n * blocks : (n + 1) * blocks, width:]
        reals.append(real * twist_real + imag * twist_imag)
        imags.append(imag * twist_real - real * twist_imag)
    grid = jnp.concatenate([jnp.concatenate(reals, axis=1), jnp.concatenate(imags, axis=1)], axis=0)
    leave = enter_ref[...].T
    if fine:
        high, low = split(grid)
        wide = dot(leave, high)
        result = wide[:blocks] + (wide[blocks:] + dot(leave[:blocks], low))
    else:
        result = dot(leave[:blocks], grid.astype(BF16))
    return result * (1.0 / (blocks * width))


def filter_side_kernel(
    got_ref, taps_ref, enter_ref, twist_ref, inner_ref,
    spectrum_ref, raw_ref, square_ref, rows_ref,
):
    blocks, lanes_in, width = got_ref.shape
    count = lanes_in // 3
    lanes_here = 2 * count
    rows_ref[...] = got_ref[:, :lanes_here].astype(F32).reshape(blocks * lanes_here, width)
    ahead = jnp.concatenate([jnp.zeros((1, width), F32), group_taps(taps_ref, count)], axis=1)
    mix_table = slide(ahead, 2 * width)[:, :width].astype(BF16)
    row = lax.broadcasted_iota(jnp.int32, (blocks, width), 0)
    pairs, columns = [], []
    for c in range(count):
        signal = channel_rows(rows_ref, c, lanes_here, blocks)
        before = jnp.where(row == 0, 0.0, pltpu.roll(signal, 1, 0))
        pairs.append(jnp.concatenate([before, signal], axis=1).astype(BF16))
        columns.append(channel_rows(rows_ref, count + c, lanes_here, blocks).astype(BF16))
    mixed = dot(jnp.concatenate(pairs, axis=0), mix_table).astype(BF16)
    highs, lows = enter_grid(columns, enter_ref, twist_ref)
    upstreams = three(highs, lows, inner_ref)
    spectrum_ref[...] = upstreams
    columns = [mixed[c * blocks : (c + 1) * blocks] for c in range(count)]
    highs, lows = enter_grid(columns, enter_ref, twist_ref)
    mixeds = three(highs, lows, inner_ref)
    lefts = [upstreams[c * blocks : (c + 1) * blocks] for c in range(count)]
    rights = [mixeds[c * blocks : (c + 1) * blocks] for c in range(count)]
    result = correlate(lefts, rights, enter_ref, twist_ref, inner_ref, False)
    squares = jnp.zeros((blocks, width), F32)
    for c in range(count):
        raw = result[:, c * width : (c + 1) * width].astype(BF16)
        raw_ref[c] = raw
        squares = squares + raw.astype(F32) * raw.astype(F32)
    total = jnp.sum(squares, axis=(0, 1), keepdims=True)
    square_ref[...] = jnp.broadcast_to(total[None], square_ref.shape)


def signal_side_kernel(
    got_ref, spectrum_ref, raw_ref, taps_ref, skip_ref, enter_ref, twist_ref, inner_ref,
    out_ref, short_ref, rows_ref, made_ref,
):
    blocks, pairs_out, _, width = out_ref.shape
    count = pairs_out - 1
    lanes_in = 3 * count
    rows_ref[...] = got_ref[...].astype(F32).reshape(blocks * lanes_in, width)
    behind = jnp.concatenate([group_taps(taps_ref, count), jnp.zeros((1, width), F32)], axis=1)
    unmix_table = slide(behind, width).astype(BF16)
    row = lax.broadcasted_iota(jnp.int32, (blocks, width), 0)
    columns = [channel_rows(rows_ref, 2 * count + c, lanes_in, blocks).astype(BF16) for c in range(count)]
    highs, lows = enter_grid(columns, enter_ref, twist_ref)
    spectra = three(highs, lows, inner_ref)
    lefts = [spectrum_ref[c * blocks : (c + 1) * blocks, :] for c in range(count)]
    rights = [spectra[c * blocks : (c + 1) * blocks] for c in range(count)]
    result = correlate(lefts, rights, enter_ref, twist_ref, inner_ref, True)
    first = lax.axis_index("seq") * count
    pairs, grads, signals = [], [], []
    for c in range(count):
        upstream = channel_rows(rows_ref, count + c, lanes_in, blocks)
        grad = (skip_ref[first + c] * upstream + result[:, c * width : (c + 1) * width]).astype(BF16)
        after = jnp.where(row == blocks - 1, 0.0, pltpu.roll(grad.astype(F32), blocks - 1, 0))
        pairs.append(jnp.concatenate([grad, after.astype(BF16)], axis=1))
        grads.append(grad)
        signal = channel_rows(rows_ref, c, lanes_in, blocks)
        before = jnp.where(row == 0, 0.0, pltpu.roll(signal, 1, 0))
        signals.append(jnp.concatenate([before, signal], axis=1).astype(BF16))
    made = dot(jnp.concatenate(pairs, axis=0), unmix_table, ((1,), (1,)))
    for c in range(count):
        made_ref[pl.ds(c, blocks, stride=2 * count), :] = raw_ref[c].astype(F32)
        made_ref[pl.ds(count + c, blocks, stride=2 * count), :] = made[c * blocks : (c + 1) * blocks]
    out_ref[:, :count] = made_ref[...].reshape(blocks, count, 2, width).astype(BF16)
    out_ref[:, count:] = jnp.zeros((blocks, 1, 2, width), BF16)
    table = dot(jnp.concatenate(grads, axis=0), jnp.concatenate(signals, axis=0), ((0,), (0,)))
    turned = table.T
    source = lax.broadcasted_iota(jnp.int32, turned.shape, 0)
    place = lax.broadcasted_iota(jnp.int32, turned.shape, 1)
    inside = jnp.logical_and(place < source, source <= place + width)
    lined = skew(jnp.where(inside, turned, 0.0), -1)
    short_ref[...] = jnp.broadcast_to(jnp.sum(lined, axis=0, keepdims=True), short_ref.shape)


def filter_side(got, taps, tables, slabs):
    blocks, lanes_in, width = got.shape
    count = lanes_in // 3
    vmem = pl.BlockSpec(memory_space=pltpu.VMEM)
    return pl.pallas_call(
        filter_side_kernel,
        out_shape=(
            jax.ShapeDtypeStruct((count * blocks, 2 * width), F32),
            jax.ShapeDtypeStruct((count, blocks, width), BF16),
            jax.ShapeDtypeStruct((slabs, 1, width), F32),
        ),
        in_specs=[vmem] * 5,
        out_specs=(vmem,) * 3,
        scratch_shapes=[
            pltpu.VMEM((blocks * 2 * count, width), F32),
        ],
        compiler_params=pltpu.CompilerParams(vmem_limit_bytes=40 * 2**20),
        cost_estimate=pl.CostEstimate(flops=3 * 10**9, bytes_accessed=6 * 10**6, transcendentals=0),
    )(got, taps, *tables)


def signal_side(got, spectrum, raw, taps, skip, tables):
    blocks, lanes_in, width = got.shape
    count = lanes_in // 3
    vmem = pl.BlockSpec(memory_space=pltpu.VMEM)
    return pl.pallas_call(
        signal_side_kernel,
        out_shape=(
            jax.ShapeDtypeStruct((blocks, count + 1, 2, width), BF16),
            jax.ShapeDtypeStruct((8, width), F32),
        ),
        in_specs=[vmem] * 4 + [pl.BlockSpec(memory_space=pltpu.SMEM)] + [vmem] * 3,
        out_specs=(vmem, vmem),
        scratch_shapes=[
            pltpu.VMEM((blocks * lanes_in, width), F32),
            pltpu.VMEM((blocks * 2 * count, width), F32),
        ],
        compiler_params=pltpu.CompilerParams(vmem_limit_bytes=40 * 2**20),
        cost_estimate=pl.CostEstimate(flops=3 * 10**9, bytes_accessed=6 * 10**6, transcendentals=0),
    )(got, spectrum, raw, taps, skip, *tables)


def stamp_kernel(message_ref, short_ref, squares_ref, out_ref, extra_ref, sem):
    del message_ref
    blocks, _, width = extra_ref.shape
    short = short_ref[:1, :]
    short_high = short.astype(BF16).astype(F32)
    square = jnp.sum(squares_ref[...], axis=0)[:1, :]
    square_high = square.astype(BF16).astype(F32)
    lane = lax.broadcasted_iota(jnp.int32, (1, width), 1)
    rest = jnp.where(lane == 0, square_high, jnp.where(lane == 1, square - square_high, short - short_high))
    both = jnp.concatenate([short_high, rest], axis=0)
    extra_ref[...] = jnp.broadcast_to(both[None], extra_ref.shape).astype(BF16)
    copy = pltpu.make_async_copy(extra_ref, out_ref.at[:, out_ref.shape[1] - 1], sem)
    copy.start()
    copy.wait()


def stamp(message, short, squares):
    blocks, _, _, width = message.shape
    vmem = pl.BlockSpec(memory_space=pltpu.VMEM)
    hbm = pl.BlockSpec(memory_space=pl.ANY)
    return pl.pallas_call(
        stamp_kernel,
        out_shape=jax.ShapeDtypeStruct(message.shape, BF16),
        in_specs=[hbm, vmem, vmem],
        out_specs=hbm,
        input_output_aliases={0: 0},
        scratch_shapes=[pltpu.VMEM((blocks, 2, width), BF16), pltpu.SemaphoreType.DMA],
        compiler_params=pltpu.CompilerParams(vmem_limit_bytes=8 * 2**20),
    )(message, short, squares)


def pack_kernel(first_ref, second_ref, third_ref, out_ref, held_ref, sems):
    owners, lanes_out, rows = out_ref.shape
    count = lanes_out // 3
    copies = [
        pltpu.make_async_copy(ref, held_ref.at[i], sems.at[i])
        for i, ref in enumerate((first_ref, second_ref, third_ref))
    ]
    for copy in copies:
        copy.start()
    for i, copy in enumerate(copies):
        copy.wait()
        out_ref[:, i * count : (i + 1) * count, :] = held_ref[i].T.reshape(owners, count, rows)


def pack(first, second, third, owners):
    rows, channels = first.shape
    hbm = pl.BlockSpec(memory_space=pl.ANY)
    first, second, third = [pltpu.with_memory_space_constraint(x, pltpu.HBM) for x in (first, second, third)]
    return pl.pallas_call(
        pack_kernel,
        out_shape=jax.ShapeDtypeStruct((owners, 3 * channels // owners, rows), BF16),
        in_specs=[hbm] * 3,
        out_specs=pl.BlockSpec(memory_space=pltpu.VMEM),
        scratch_shapes=[pltpu.VMEM((3, rows, channels), BF16), pltpu.SemaphoreType.DMA((3,))],
        compiler_params=pltpu.CompilerParams(vmem_limit_bytes=16 * 2**20),
        cost_estimate=pl.CostEstimate(flops=10**6, bytes_accessed=6 * rows * channels * 2, transcendentals=0),
    )(first, second, third)


def finish_kernel(entries, scale, back_ref, signal_ref, filter_ref, short_ref):
    parts, pairs, _, rows = back_ref.shape
    half = (pairs - 1) // 2
    channels = signal_ref.shape[1]
    groups = short_ref.shape[0]
    extra = back_ref[:, pairs - 1].astype(F32)
    high, low = extra[:, 0], extra[:, 1]
    lane = lax.broadcasted_iota(jnp.int32, low.shape, 1)
    short = high + jnp.where(lane < 2, 0.0, low)
    short_ref[...] = jnp.sum(short.reshape(groups, parts // groups, rows), axis=1) * scale
    squares = jnp.sum(jnp.where(lane < 2, low, 0.0), axis=(0, 1), keepdims=True)
    divisor = jnp.maximum(1.0, jnp.sqrt(squares * (1.0 / entries)))
    signal_ref[...] = back_ref[:, half : 2 * half].reshape(channels, rows).T
    raw = back_ref[:, :half].astype(F32).reshape(channels, rows)
    filter_ref[...] = (raw / divisor).astype(BF16).T


def finish(back, channels, groups, entries, scale):
    rows = back.shape[3]
    vmem = pl.BlockSpec(memory_space=pltpu.VMEM)
    return pl.pallas_call(
        lambda *refs: finish_kernel(entries, scale, *refs),
        out_shape=(
            jax.ShapeDtypeStruct((rows, channels), BF16),
            jax.ShapeDtypeStruct((rows, channels), BF16),
            jax.ShapeDtypeStruct((groups, rows), F32),
        ),
        in_specs=[vmem],
        out_specs=(vmem, vmem, vmem),
        compiler_params=pltpu.CompilerParams(vmem_limit_bytes=16 * 2**20),
    )(back)


def on_device(signal, upstream, long_filter, short_filter, skip_gain):
    rows, channels = signal.shape
    parts = lax.axis_size("seq")
    slabs = lax.axis_size("ch")
    count = channels // parts
    groups = short_filter.shape[1]
    tables = [jnp.asarray(table) for table in dft_tables(parts, rows)]

    got = lax.all_to_all(pack(signal, upstream, long_filter, parts), "seq", 0, 0, tiled=True)
    taps = short_filter.T
    spectrum, raw, squares = filter_side(got, taps, tables, slabs)
    squares = lax.all_to_all(squares, "ch", 0, 0, tiled=True)
    message, short = signal_side(got, spectrum, raw, taps, skip_gain, tables)
    back = lax.all_to_all(stamp(message, short, squares), "seq", 0, 0, tiled=True)
    entries = float(rows * parts * channels * slabs)
    scale = 1.0 / math.sqrt(GROUP * rows * parts)
    grad_signal, grad_long, short = finish(back, channels, groups, entries, scale)
    return (grad_signal, grad_long, short.T)


def solution(mesh):
    placed = (P("seq", "ch"), P("seq", "ch"), P("seq", "ch"), P(None, "ch"), P("ch"))
    return jax.shard_map(
        on_device,
        mesh=mesh,
        in_specs=placed,
        out_specs=(P("seq", "ch"), P("seq", "ch"), P(None, "ch")),
        check_vma=False,
    )
```

```python
import math

import jax
import jax.numpy as jnp
import numpy as np
from jax import lax
from jax.experimental import pallas as pl
from jax.experimental.pallas import tpu as pltpu
from jax.sharding import PartitionSpec as P

GROUP = 16
F32 = jnp.float32
BF16 = jnp.bfloat16


def split_table(table):
    high = table.astype(BF16)
    low = (table - high.astype(np.float64)).astype(BF16)
    return high, low


def dft_tables(blocks, width):
    total = 2 * blocks * width
    k1 = np.arange(blocks)[:, None] + 0.5
    b = np.arange(blocks)[None, :]
    p = np.arange(width)[None, :]
    angle = 2.0 * np.pi * k1 * b / (2 * blocks)
    enter = np.concatenate([np.cos(angle), -np.sin(angle)], axis=0)
    enter_high, enter_low = split_table(enter)
    enter_both = np.concatenate([enter_high, enter_low], axis=1)
    twist_angle = 2.0 * np.pi * k1 * p / total
    twist = np.stack([np.cos(twist_angle), -np.sin(twist_angle)]).astype(np.float32)
    inner_angle = 2.0 * np.pi * np.arange(width)[:, None] * p / width
    cosine, sine = np.cos(inner_angle), np.sin(inner_angle)
    inner = np.block([[cosine, -sine], [sine, cosine]])
    return enter_both, twist, np.stack(split_table(inner))


def split(value):
    high = value.astype(BF16)
    return high, (value - high.astype(F32)).astype(BF16)


def dot(left, right, dims=((1,), (0,))):
    return lax.dot_general(left, right, (dims, ((), ())), preferred_element_type=F32)


def skew(value, step):
    rows, width = value.shape
    row = lax.broadcasted_iota(jnp.int32, value.shape, 0)
    bit = 1
    while bit < rows:
        moved = pltpu.roll(value, (bit * step) % width, 1)
        value = jnp.where((row & bit) != 0, moved, value)
        bit *= 2
    return value


def group_taps(taps_ref, count):
    group = lax.axis_index("seq") * count // GROUP
    row = lax.broadcasted_iota(jnp.int32, taps_ref.shape, 0)
    return jnp.sum(jnp.where(row == group, taps_ref[...].astype(F32), 0.0), axis=0, keepdims=True)


def slide(line, rows):
    return pltpu.roll(jnp.broadcast_to(line, (rows, line.shape[1])), 0, 1, stride=1, stride_axis=0)


def three(highs, lows, tables, dims=((1,), (0,))):
    high = jnp.concatenate(highs, axis=0)
    low = jnp.concatenate(lows, axis=0)
    return dot(high, tables[0], dims) + (dot(low, tables[0], dims) + dot(high, tables[1], dims))


def channel_rows(ref, first, stride, blocks):
    return ref[pl.ds(first, blocks, stride=stride), :]


def enter_grid(columns, enter_ref, twist_ref):
    blocks, width = columns[0].shape
    side = jnp.concatenate(columns, axis=1)
    grid = dot(enter_ref[...], jnp.concatenate([side, side], axis=0))
    twist_real, twist_imag = twist_ref[0], twist_ref[1]
    highs, lows = [], []
    for n in range(len(columns)):
        real = grid[:blocks, n * width : (n + 1) * width]
        imag = grid[blocks:, n * width : (n + 1) * width]
        high, low = split(
            jnp.concatenate(
                [real * twist_real - imag * twist_imag, real * twist_imag + imag * twist_real], axis=1
            )
        )
        highs.append(high)
        lows.append(low)
    return highs, lows


def correlate(lefts, rights, enter_ref, twist_ref, inner_ref, fine):
    blocks = lefts[0].shape[0]
    width = lefts[0].shape[1] // 2
    twist_real, twist_imag = twist_ref[0], twist_ref[1]
    transposed = ((1,), (1,))
    products = []
    for left, right in zip(lefts, rights):
        left_real, left_imag = left[:, :width], left[:, width:]
        real, imag = right[:, :width], right[:, width:]
        products.append(
            jnp.concatenate(
                [left_real * real + left_imag * imag, left_imag * real - left_real * imag], axis=1
            )
        )
    if fine:
        highs, lows = zip(*[split(product) for product in products])
        backs = three(highs, lows, inner_ref, transposed)
    else:
        high = jnp.concatenate([product.astype(BF16) for product in products], axis=0)
        backs = dot(high, inner_ref[0], transposed)
    reals, imags = [], []
    for n in range(len(lefts)):
        real = backs[n * blocks : (n + 1) * blocks, :width]
        imag = backs[n * blocks : (n + 1) * blocks, width:]
        reals.append(real * twist_real + imag * twist_imag)
        imags.append(imag * twist_real - real * twist_imag)
    grid = jnp.concatenate([jnp.concatenate(reals, axis=1), jnp.concatenate(imags, axis=1)], axis=0)
    if fine:
        leave = enter_ref[...].T
        high, low = split(grid)
        wide = dot(leave, high)
        result = wide[:blocks] + (wide[blocks:] + dot(leave[:blocks], low))
    else:
        result = dot(enter_ref[:, :blocks].T, grid.astype(BF16))
    return result * (1.0 / (blocks * width))


def filter_side_kernel(
    got_ref, taps_ref, enter_ref, twist_ref, inner_ref,
    spectrum_ref, raw_ref, square_ref, rows_ref,
):
    blocks, lanes_in, width = got_ref.shape
    count = lanes_in // 3
    lanes_here = 2 * count
    rows_ref[...] = got_ref[:, :lanes_here].astype(F32).reshape(blocks * lanes_here, width)
    ahead = jnp.concatenate([jnp.zeros((1, width), F32), group_taps(taps_ref, count)], axis=1)
    mix_table = slide(ahead, 2 * width)[:, :width].astype(BF16)
    row = lax.broadcasted_iota(jnp.int32, (blocks, width), 0)
    pairs, columns = [], []
    for c in range(count):
        signal = channel_rows(rows_ref, c, lanes_here, blocks)
        before = jnp.where(row == 0, 0.0, pltpu.roll(signal, 1, 0))
        pairs.append(jnp.concatenate([before, signal], axis=1).astype(BF16))
        columns.append(channel_rows(rows_ref, count + c, lanes_here, blocks).astype(BF16))
    mixed = dot(jnp.concatenate(pairs, axis=0), mix_table).astype(BF16)
    highs, lows = enter_grid(columns, enter_ref, twist_ref)
    upstreams = three(highs, lows, inner_ref)
    spectrum_ref[...] = upstreams
    columns = [mixed[c * blocks : (c + 1) * blocks] for c in range(count)]
    highs, lows = enter_grid(columns, enter_ref, twist_ref)
    mixeds = three(highs, lows, inner_ref)
    lefts = [upstreams[c * blocks : (c + 1) * blocks] for c in range(count)]
    rights = [mixeds[c * blocks : (c + 1) * blocks] for c in range(count)]
    result = correlate(lefts, rights, enter_ref, twist_ref, inner_ref, False)
    squares = jnp.zeros((blocks, width), F32)
    for c in range(count):
        raw = result[:, c * width : (c + 1) * width].astype(BF16)
        raw_ref[c] = raw
        squares = squares + raw.astype(F32) * raw.astype(F32)
    total = jnp.sum(squares, axis=(0, 1), keepdims=True)
    square_ref[...] = jnp.broadcast_to(total[None], square_ref.shape)


def signal_side_kernel(
    got_ref, spectrum_ref, raw_ref, taps_ref, skip_ref, enter_ref, twist_ref, inner_ref,
    out_ref, short_ref, rows_ref, made_ref,
):
    blocks, pairs_out, _, width = out_ref.shape
    count = pairs_out - 1
    lanes_in = 3 * count
    rows_ref[...] = got_ref[...].astype(F32).reshape(blocks * lanes_in, width)
    behind = jnp.concatenate([group_taps(taps_ref, count), jnp.zeros((1, width), F32)], axis=1)
    unmix_table = slide(behind, width).astype(BF16)
    row = lax.broadcasted_iota(jnp.int32, (blocks, width), 0)
    columns = [channel_rows(rows_ref, 2 * count + c, lanes_in, blocks).astype(BF16) for c in range(count)]
    highs, lows = enter_grid(columns, enter_ref, twist_ref)
    spectra = three(highs, lows, inner_ref)
    lefts = [spectrum_ref[c * blocks : (c + 1) * blocks, :] for c in range(count)]
    rights = [spectra[c * blocks : (c + 1) * blocks] for c in range(count)]
    result = correlate(lefts, rights, enter_ref, twist_ref, inner_ref, True)
    first = lax.axis_index("seq") * count
    pairs, grads, signals = [], [], []
    for c in range(count):
        upstream = channel_rows(rows_ref, count + c, lanes_in, blocks)
        grad = (skip_ref[first + c] * upstream + result[:, c * width : (c + 1) * width]).astype(BF16)
        after = jnp.where(row == blocks - 1, 0.0, pltpu.roll(grad.astype(F32), blocks - 1, 0))
        pairs.append(jnp.concatenate([grad, after.astype(BF16)], axis=1))
        grads.append(grad)
        signal = channel_rows(rows_ref, c, lanes_in, blocks)
        before = jnp.where(row == 0, 0.0, pltpu.roll(signal, 1, 0))
        signals.append(jnp.concatenate([before, signal], axis=1).astype(BF16))
    made = dot(jnp.concatenate(pairs, axis=0), unmix_table, ((1,), (1,)))
    for c in range(count):
        made_ref[pl.ds(c, blocks, stride=2 * count), :] = raw_ref[c].astype(F32)
        made_ref[pl.ds(count + c, blocks, stride=2 * count), :] = made[c * blocks : (c + 1) * blocks]
    out_ref[:, :count] = made_ref[...].reshape(blocks, count, 2, width).astype(BF16)
    out_ref[:, count:] = jnp.zeros((blocks, 1, 2, width), BF16)
    table = dot(jnp.concatenate(grads, axis=0), jnp.concatenate(signals, axis=0), ((0,), (0,)))
    turned = table.T
    source = lax.broadcasted_iota(jnp.int32, turned.shape, 0)
    place = lax.broadcasted_iota(jnp.int32, turned.shape, 1)
    inside = jnp.logical_and(place < source, source <= place + width)
    lined = skew(jnp.where(inside, turned, 0.0), -1)
    short_ref[...] = jnp.broadcast_to(jnp.sum(lined, axis=0, keepdims=True), short_ref.shape)


def filter_side(got, taps, tables, slabs):
    blocks, lanes_in, width = got.shape
    count = lanes_in // 3
    vmem = pl.BlockSpec(memory_space=pltpu.VMEM)
    return pl.pallas_call(
        filter_side_kernel,
        out_shape=(
            jax.ShapeDtypeStruct((count * blocks, 2 * width), F32),
            jax.ShapeDtypeStruct((count, blocks, width), BF16),
            jax.ShapeDtypeStruct((slabs, 1, width), F32),
        ),
        in_specs=[vmem] * 5,
        out_specs=(vmem,) * 3,
        scratch_shapes=[
            pltpu.VMEM((blocks * 2 * count, width), F32),
        ],
        compiler_params=pltpu.CompilerParams(vmem_limit_bytes=40 * 2**20),
        cost_estimate=pl.CostEstimate(flops=3 * 10**9, bytes_accessed=6 * 10**6, transcendentals=0),
    )(got, taps, *tables)


def signal_side(got, spectrum, raw, taps, skip, tables):
    blocks, lanes_in, width = got.shape
    count = lanes_in // 3
    vmem = pl.BlockSpec(memory_space=pltpu.VMEM)
    return pl.pallas_call(
        signal_side_kernel,
        out_shape=(
            jax.ShapeDtypeStruct((blocks, count + 1, 2, width), BF16),
            jax.ShapeDtypeStruct((8, width), F32),
        ),
        in_specs=[vmem] * 4 + [pl.BlockSpec(memory_space=pltpu.SMEM)] + [vmem] * 3,
        out_specs=(vmem, vmem),
        scratch_shapes=[
            pltpu.VMEM((blocks * lanes_in, width), F32),
            pltpu.VMEM((blocks * 2 * count, width), F32),
        ],
        compiler_params=pltpu.CompilerParams(vmem_limit_bytes=40 * 2**20),
        cost_estimate=pl.CostEstimate(flops=3 * 10**9, bytes_accessed=6 * 10**6, transcendentals=0),
    )(got, spectrum, raw, taps, skip, *tables)


def stamp_kernel(message_ref, short_ref, squares_ref, out_ref, extra_ref, sem):
    del message_ref
    blocks, _, width = extra_ref.shape
    short = short_ref[:1, :]
    short_high = short.astype(BF16).astype(F32)
    square = jnp.sum(squares_ref[...], axis=0)[:1, :]
    square_high = square.astype(BF16).astype(F32)
    lane = lax.broadcasted_iota(jnp.int32, (1, width), 1)
    rest = jnp.where(lane == 0, square_high, jnp.where(lane == 1, square - square_high, short - short_high))
    both = jnp.concatenate([short_high, rest], axis=0)
    extra_ref[...] = jnp.broadcast_to(both[None], extra_ref.shape).astype(BF16)
    copy = pltpu.make_async_copy(extra_ref, out_ref.at[:, out_ref.shape[1] - 1], sem)
    copy.start()
    copy.wait()


def stamp(message, short, squares):
    blocks, _, _, width = message.shape
    vmem = pl.BlockSpec(memory_space=pltpu.VMEM)
    hbm = pl.BlockSpec(memory_space=pl.ANY)
    return pl.pallas_call(
        stamp_kernel,
        out_shape=jax.ShapeDtypeStruct(message.shape, BF16),
        in_specs=[hbm, vmem, vmem],
        out_specs=hbm,
        input_output_aliases={0: 0},
        scratch_shapes=[pltpu.VMEM((blocks, 2, width), BF16), pltpu.SemaphoreType.DMA],
        compiler_params=pltpu.CompilerParams(vmem_limit_bytes=8 * 2**20),
    )(message, short, squares)


def pack_kernel(first_ref, second_ref, third_ref, out_ref, held_ref, sems):
    owners, lanes_out, rows = out_ref.shape
    count = lanes_out // 3
    copies = [
        pltpu.make_async_copy(ref, held_ref.at[i], sems.at[i])
        for i, ref in enumerate((first_ref, second_ref, third_ref))
    ]
    for copy in copies:
        copy.start()
    for i, copy in enumerate(copies):
        copy.wait()
        out_ref[:, i * count : (i + 1) * count, :] = held_ref[i].T.reshape(owners, count, rows)


def pack(first, second, third, owners):
    rows, channels = first.shape
    hbm = pl.BlockSpec(memory_space=pl.ANY)
    first, second, third = [pltpu.with_memory_space_constraint(x, pltpu.HBM) for x in (first, second, third)]
    return pl.pallas_call(
        pack_kernel,
        out_shape=jax.ShapeDtypeStruct((owners, 3 * channels // owners, rows), BF16),
        in_specs=[hbm] * 3,
        out_specs=pl.BlockSpec(memory_space=pltpu.VMEM),
        scratch_shapes=[pltpu.VMEM((3, rows, channels), BF16), pltpu.SemaphoreType.DMA((3,))],
        compiler_params=pltpu.CompilerParams(vmem_limit_bytes=16 * 2**20),
        cost_estimate=pl.CostEstimate(flops=10**6, bytes_accessed=6 * rows * channels * 2, transcendentals=0),
    )(first, second, third)


def finish_kernel(entries, scale, back_ref, signal_ref, filter_ref, short_ref):
    parts, pairs, _, rows = back_ref.shape
    half = (pairs - 1) // 2
    channels = signal_ref.shape[1]
    groups = short_ref.shape[0]
    extra = back_ref[:, pairs - 1].astype(F32)
    high, low = extra[:, 0], extra[:, 1]
    lane = lax.broadcasted_iota(jnp.int32, low.shape, 1)
    short = high + jnp.where(lane < 2, 0.0, low)
    short_ref[...] = jnp.sum(short.reshape(groups, parts // groups, rows), axis=1) * scale
    squares = jnp.sum(jnp.where(lane < 2, low, 0.0), axis=(0, 1), keepdims=True)
    divisor = jnp.maximum(1.0, jnp.sqrt(squares * (1.0 / entries)))
    signal_ref[...] = back_ref[:, half : 2 * half].reshape(channels, rows).T
    raw = back_ref[:, :half].astype(F32).reshape(channels, rows)
    filter_ref[...] = (raw / divisor).astype(BF16).T


def finish(back, channels, groups, entries, scale):
    rows = back.shape[3]
    vmem = pl.BlockSpec(memory_space=pltpu.VMEM)
    return pl.pallas_call(
        lambda *refs: finish_kernel(entries, scale, *refs),
        out_shape=(
            jax.ShapeDtypeStruct((rows, channels), BF16),
            jax.ShapeDtypeStruct((rows, channels), BF16),
            jax.ShapeDtypeStruct((groups, rows), F32),
        ),
        in_specs=[vmem],
        out_specs=(vmem, vmem, vmem),
        compiler_params=pltpu.CompilerParams(vmem_limit_bytes=16 * 2**20),
    )(back)


def on_device(signal, upstream, long_filter, short_filter, skip_gain):
    rows, channels = signal.shape
    parts = lax.axis_size("seq")
    slabs = lax.axis_size("ch")
    count = channels // parts
    groups = short_filter.shape[1]
    tables = [jnp.asarray(table) for table in dft_tables(parts, rows)]

    got = lax.all_to_all(pack(signal, upstream, long_filter, parts), "seq", 0, 0, tiled=True)
    taps = short_filter.T
    spectrum, raw, squares = filter_side(got, taps, tables, slabs)
    squares = lax.all_to_all(squares, "ch", 0, 0, tiled=True)
    message, short = signal_side(got, spectrum, raw, taps, skip_gain, tables)
    back = lax.all_to_all(stamp(message, short, squares), "seq", 0, 0, tiled=True)
    entries = float(rows * parts * channels * slabs)
    scale = 1.0 / math.sqrt(GROUP * rows * parts)
    grad_signal, grad_long, short = finish(back, channels, groups, entries, scale)
    return (grad_signal, grad_long, short.T)


def solution(mesh):
    placed = (P("seq", "ch"), P("seq", "ch"), P("seq", "ch"), P(None, "ch"), P("ch"))
    return jax.shard_map(
        on_device,
        mesh=mesh,
        in_specs=placed,
        out_specs=(P("seq", "ch"), P("seq", "ch"), P(None, "ch")),
        check_vma=False,
    )
```
